512 devices in a mesh: ctx: 16 (over y, x), sp: 32 (over z, core).
Axes of the slice: x: 4, y: 4, z: 16, core: 2. Of those that a mesh axis runs over, the one named last changes fastest.
Arguments:
- query_rows: bfloat16 [65536, 2048], P(('ctx', 'sp')), may hold values from -6 to 6
- key_rows: bfloat16 [65536, 2048], P(('ctx', 'sp')), may hold values from -6 to 6
- value_rows: bfloat16 [65536, 2048], P(('ctx', 'sp')), may hold values from -6 to 6
- out_grad: bfloat16 [65536, 2048], P(('ctx', 'sp')), may hold values from -6 to 6
- positions: int32 [65536], P(('ctx', 'sp')), may hold values from 0 to 4095, as said below
Outputs:
- query_grad: bfloat16 [65536, 2048], P(('ctx', 'sp'))
- key_grad: bfloat16 [65536, 2048], P(('ctx', 'sp'))
- value_grad: bfloat16 [65536, 2048], P(('ctx', 'sp'))
The draws below stay inside these ranges and needn't reach their ends.
Inputs may be any that keep to these rules, and one draw needn't show every extreme that they name: `positions`: each token's position within its document, 0 at a document's first token and rising by one per token; a document starts at least at the first token of every group of 128 * 32 consecutive tokens, and the first such group is one whole document.
All inputs are finite; a program needn't handle non-finite values.
Results may differ from the reference program's by a relative error of at most 0.0063.
Values may be sent and summed in bfloat16 or wider, within the bound.
No kernel may reach another device: no remote copies, remote signals or barrier semaphores. Data moves between devices by JAX's collectives and lax.ppermute only.
A program may use at most 64 MiB of HBM per device.

```python
import math
from functools import partial
import jax
import jax.numpy as jnp
from jax import lax

H = 32
HD = 64
SPAN = 128
TOK_DEV = 128
TOKENS = 65536
N_CTX = 16
N_SP = 32


def draw_positions(key, part):
    key = jax.random.fold_in(key, 7)
    number = TOK_DEV * N_CTX * N_SP
    group_len = TOK_DEV * N_SP
    rate = max(16, group_len // 8)
    places = jnp.arange(number, dtype=jnp.int32)
    random_starts = (jax.random.randint(key, (number,), 0, rate) == 0) & (places >= group_len)
    starts = random_starts | (places % group_len == 0)
    latest = lax.cummax(jnp.where(starts, places, 0), axis=0)
    return (places - latest).astype(jnp.int32)


def steps_of(rng, extent, cuts, smallest, high):
    def one(axis_at, shards_of):
        steps = jax.random.uniform(jax.random.fold_in(jax.random.fold_in(rng, 6), axis_at), (shards_of,), jnp.float32, smallest / len(cuts), high / len(cuts))
        return jnp.repeat(jnp.exp(steps), extent[axis_at] // shards_of).reshape((-1,) + (1,) * (len(extent) - axis_at - 1))

    level = one(*cuts[0])
    for cut in cuts[1:]:
        level = level * one(*cut)
    return level


def scatter_about(stream_key, shape, deviation, bound, shards=(), kind=jnp.bfloat16):
    result = deviation * jax.random.normal(stream_key, shape, jnp.float32)
    if shards:
        result = result * steps_of(stream_key, shape, shards, -0.22, 0.18)
    return jnp.clip(result, -bound, bound).astype(kind)


def setup_inputs(seed: int = 0) -> dict:
    seeds = jax.random.split(jax.random.key(seed), 6)
    return {
        "query_rows": scatter_about(seeds[0], (TOKENS, H * HD), 1.0, 6.0, ((0, 512),)),
        "key_rows": scatter_about(seeds[1], (TOKENS, H * HD), 1.0, 6.0, ((0, 512),)),
        "value_rows": scatter_about(seeds[2], (TOKENS, H * HD), 1.0, 6.0, ((0, 512),)),
        "out_grad": scatter_about(seeds[3], (TOKENS, H * HD), 1.0, 6.0, ((0, 512),)),
        "positions": draw_positions(jax.random.fold_in(seeds[5], 71), 0),
    }


BASE = 500000.0

def rotate(rows, positions, direction):
    number = rows.shape[0]
    head_count = rows.shape[1] // HD
    half = HD // 2
    frequency = BASE ** (-jnp.arange(half, dtype=jnp.float32) / half)
    angles = positions.astype(jnp.float32)[:, None] * frequency[None, :]
    cosine = jnp.cos(angles)[:, None, :]
    sine_table = jnp.sin(angles)[:, None, :]
    halves = rows.astype(jnp.float32).reshape(number, head_count, 2, half)
    lower_half = halves[:, :, 0]
    upper_half = halves[:, :, 1]
    new_lower = lower_half * cosine - direction * upper_half * sine_table
    new_upper = upper_half * cosine + direction * lower_half * sine_table
    return jnp.stack([new_lower, new_upper], axis=2).reshape(number, head_count * HD)

def widen(value):
    return lax.optimization_barrier(value.astype(jnp.bfloat16)).astype(jnp.float32)

def one_block(factor, pieces):
    query_b, key_b, value_b, grad_b, before, later_sum = pieces
    query_f = query_b.astype(jnp.float32)
    key_f = key_b.astype(jnp.float32)
    value_f = value_b.astype(jnp.float32)
    grad_f = grad_b.astype(jnp.float32)
    length = query_b.shape[0]
    causal = (jnp.arange(length)[:, None] >= jnp.arange(length)[None, :])[None]
    hp = lax.Precision.HIGHEST
    grad_scores = jnp.einsum('thb,shb->hts', grad_f, value_f, precision=hp)
    key_scores = jnp.einsum('tha,sha->hts', query_f, key_f, precision=hp)
    weights = widen(factor * jnp.where(causal, grad_scores, 0.0))
    key_low = widen(factor * jnp.where(causal, key_scores, 0.0))
    state_low = widen(factor * before)
    grad_low = widen(factor * later_sum)
    query_out = jnp.einsum('hts,sha->tha', weights, key_f, precision=hp) + jnp.einsum('thb,hab->tha', grad_f, state_low, precision=hp)
    key_out = jnp.einsum('hts,tha->sha', weights, query_f, precision=hp) + jnp.einsum('shb,hab->sha', value_f, grad_low, precision=hp)
    value_out = jnp.einsum('hts,thb->shb', key_low, grad_f, precision=hp) + jnp.einsum('sha,hab->shb', key_f, grad_low, precision=hp)
    return (query_out.astype(jnp.bfloat16), key_out.astype(jnp.bfloat16), value_out.astype(jnp.bfloat16))

def per_head(factor, arrays):
    query_h, key_h, value_h, grad_h = arrays
    hp = lax.Precision.HIGHEST
    state_terms = jnp.einsum('ncha,nchb->nhab', key_h.astype(jnp.float32), value_h.astype(jnp.float32), precision=hp)
    grad_terms = jnp.einsum('ncha,nchb->nhab', query_h.astype(jnp.float32), grad_h.astype(jnp.float32), precision=hp)
    zeros_block = jnp.zeros_like(state_terms[:1])
    before = jnp.concatenate([zeros_block, jnp.cumsum(state_terms, axis=0)[:-1]], axis=0)
    later_sum = jnp.concatenate([jnp.cumsum(grad_terms[::-1], axis=0)[::-1][1:], zeros_block], axis=0)
    return lax.map(partial(one_block, factor), (query_h, key_h, value_h, grad_h, before, later_sum))

def reference(query_rows, key_rows, value_rows, out_grad, positions):
    seq_total = query_rows.shape[0]
    head_count = query_rows.shape[1] // HD
    blocks = seq_total // SPAN
    factor = 1.0 / math.sqrt(HD * seq_total)
    query_rot = rotate(query_rows, positions, 1.0).astype(jnp.bfloat16)
    key_rot = rotate(key_rows, positions, 1.0).astype(jnp.bfloat16)

    def to_heads(rows):
        return rows.reshape(blocks, SPAN, head_count, HD).transpose(2, 0, 1, 3)[:, :, :, None, :]

    def to_rows(heads_arr):
        return heads_arr[:, :, :, 0, :].transpose(1, 2, 0, 3).reshape(seq_total, head_count * HD)
    outputs = lax.map(partial(per_head, factor), (to_heads(query_rot), to_heads(key_rot), to_heads(value_rows), to_heads(out_grad)))
    query_grad = rotate(to_rows(outputs[0]), positions, -1.0).astype(jnp.bfloat16)
    key_grad = rotate(to_rows(outputs[1]), positions, -1.0).astype(jnp.bfloat16)
    value_grad = to_rows(outputs[2])
    return (query_grad, key_grad, value_grad)
```

```python
import functools
import math

import jax
import jax.numpy as jnp
import numpy as np
from jax import lax
from jax.experimental import pallas as pl
from jax.experimental.pallas import tpu as pltpu
from jax.sharding import Mesh, PartitionSpec as P

HD = 64
SPAN = 128
BASE = 500000.0
PAIR = 2 * HD
F32 = jnp.float32
BF16 = jnp.bfloat16
STEP = 4
VMEM_LIMIT = 40 * 1024 * 1024

NT = (((1,), (1,)), ((), ()))
TN = (((0,), (0,)), ((), ()))
NN = (((1,), (0,)), ((), ()))


def dot(a, b, dims):
    return lax.dot_general(a, b, dims, preferred_element_type=F32)


def lanes(rows):
    return lax.broadcasted_iota(jnp.int32, (rows, PAIR), 1)


def swap_halves(x):
    first = (lanes(x.shape[0]) % HD) < HD // 2
    return jnp.where(first, pltpu.roll(x, PAIR - HD // 2, 1), pltpu.roll(x, HD // 2, 1))


def rotated(x, cosine, sine):
    x = x.astype(F32)
    return x * cosine + swap_halves(x) * sine


def by_head(x):
    first = lanes(x.shape[0]) < HD
    zero = jnp.zeros_like(x)
    return jnp.concatenate([jnp.where(first, x, zero), jnp.where(first, zero, x)], axis=0)


def pack_pair(m):
    first = lanes(HD) < HD
    return jnp.where(first, m[:HD], m[HD:])


def states_kernel(q_ref, k_ref, v_ref, g_ref, cos_ref, sin_ref, qr_ref, kr_ref, st_ref):
    cosine, sine = cos_ref[...], sin_ref[...]
    for p in range(STEP):
        at = slice(p * PAIR, (p + 1) * PAIR)
        q = rotated(q_ref[:, at], cosine, sine).astype(BF16)
        k = rotated(k_ref[:, at], cosine, sine).astype(BF16)
        qr_ref[:, at] = q
        kr_ref[:, at] = k
        state = pack_pair(dot(k, v_ref[:, at], TN)).astype(BF16)
        grad = pack_pair(dot(q, g_ref[:, at], TN)).astype(BF16)
        for r in range(2):
            st_ref[0, 2 * p + r, 0] = state[32 * r : 32 * r + 32]
            st_ref[0, 2 * p + r, 1] = grad[32 * r : 32 * r + 32]


def block_kernel(q_ref, k_ref, v_ref, g_ref, qo_ref, ko_ref, vo_ref):
    row = lax.broadcasted_iota(jnp.int32, (SPAN, 2 * SPAN), 0)
    col = lax.broadcasted_iota(jnp.int32, (SPAN, 2 * SPAN), 1) % SPAN
    lower = row >= col
    upper = row <= col
    for p in range(STEP):
        at = slice(p * PAIR, (p + 1) * PAIR)
        q, k, v, g = q_ref[:, at], k_ref[:, at], v_ref[:, at], g_ref[:, at]
        q2, k2, v2, g2 = by_head(q), by_head(k), by_head(v), by_head(g)
        w = jnp.where(lower, dot(g, v2, NT), 0.0).astype(BF16)
        wt = jnp.where(upper, dot(v, g2, NT), 0.0).astype(BF16)
        st = jnp.where(upper, dot(k, q2, NT), 0.0).astype(BF16)
        qo_ref[:, at] = dot(w, k2, NN)
        ko_ref[:, at] = dot(wt, q2, NN)
        vo_ref[:, at] = dot(st, g2, NN)


def finish_kernel(
    factor, k_ref, v_ref, g_ref, cos_ref, sin_ref, st_ref, qi_ref, ki_ref, vi_ref, qo_ref, ko_ref, vo_ref
):
    cosine, sine = cos_ref[...], -sin_ref[...]
    for p in range(STEP):
        at = slice(p * PAIR, (p + 1) * PAIR)
        k, v, g = k_ref[:, at], v_ref[:, at], g_ref[:, at]
        before = by_head(jnp.concatenate([st_ref[0, 2 * p, 0], st_ref[0, 2 * p + 1, 0]], axis=0))
        after = by_head(jnp.concatenate([st_ref[0, 2 * p, 1], st_ref[0, 2 * p + 1, 1]], axis=0))
        qo = (factor * (qi_ref[:, at] + dot(g, before, NT))).astype(BF16)
        ko = (factor * (ki_ref[:, at] + dot(v, after, NT))).astype(BF16)
        vo_ref[:, at] = (factor * (vi_ref[:, at] + dot(k, after, NN))).astype(BF16)
        qo_ref[:, at] = rotated(qo, cosine, sine).astype(BF16)
        ko_ref[:, at] = rotated(ko, cosine, sine).astype(BF16)


def totals_kernel(zr_ref, out_ref):
    state = zr_ref[0, 0].astype(F32)
    grad = zr_ref[0, 1].astype(F32)
    for z in range(1, zr_ref.shape[0]):
        state += zr_ref[z, 0].astype(F32)
        grad += zr_ref[z, 1].astype(F32)
    me = lax.axis_index("ctx")
    for j in range(out_ref.shape[0]):
        out_ref[j] = jnp.where(j > me, state, grad)


def scan_kernel(zr_ref, cx_ref, out_ref):
    me = lax.axis_index("ctx")
    state = jnp.zeros(cx_ref.shape[1:], F32)
    grad = jnp.zeros(cx_ref.shape[1:], F32)
    for j in range(cx_ref.shape[0]):
        state += jnp.where(j < me, cx_ref[j], 0.0)
        grad += jnp.where(j > me, cx_ref[j], 0.0)
    count = zr_ref.shape[0]
    for z in range(count):
        out_ref[z, 0] = state.astype(BF16)
        state += zr_ref[z, 0].astype(F32)
    for z in reversed(range(count)):
        out_ref[z, 1] = grad.astype(BF16)
        grad += zr_ref[z, 1].astype(F32)


def pair_sum_kernel(cc_ref, out_ref):
    for z in range(out_ref.shape[0]):
        out_ref[z] = (cc_ref[0, z].astype(F32) + cc_ref[1, z].astype(F32)).astype(BF16)


def spread_kernel(zb_ref, cc_ref, out_ref):
    for z in range(zb_ref.shape[0]):
        state, grad = zb_ref[z, 0], zb_ref[z, 1]
        out_ref[0, z, 0] = state
        out_ref[1, z, 0] = (state.astype(F32) + cc_ref[0, z, 0].astype(F32)).astype(BF16)
        out_ref[0, z, 1] = (grad.astype(F32) + cc_ref[1, z, 1].astype(F32)).astype(BF16)
        out_ref[1, z, 1] = grad


def whole(kernel, out_shape, *args):
    spec = pl.BlockSpec(memory_space=pltpu.VMEM)
    return pl.pallas_call(
        kernel,
        out_shape=out_shape,
        in_specs=[spec] * len(args),
        out_specs=spec,
        compiler_params=pltpu.CompilerParams(vmem_limit_bytes=VMEM_LIMIT),
    )(*args)


def on_device(query_rows, key_rows, value_rows, out_grad, positions):
    tokens, width = query_rows.shape
    n_ctx, n_z = lax.axis_size("ctx"), lax.axis_size("z")
    seq_total = tokens * n_ctx * n_z * lax.axis_size("core")
    factor = 1.0 / math.sqrt(HD * seq_total)
    half = HD // 2
    frequency = BASE ** (-jnp.arange(half, dtype=F32) / half)
    frequency = jnp.tile(frequency, PAIR // half)
    sign = jnp.asarray(np.tile(np.repeat(np.float32([-1.0, 1.0]), half), 2))
    angles = positions.astype(F32)[:, None] * frequency[None, :]
    cosine, sine = jnp.cos(angles), jnp.sin(angles) * sign[None, :]

    pairs = width // PAIR
    steps = pairs // STEP
    slots = 2 * pairs // 2
    rows = pl.BlockSpec((tokens, STEP * PAIR), lambda i: (0, i))
    table = pl.BlockSpec((tokens, PAIR), lambda i: (0, 0))
    per_half = steps // 2
    chunk = pl.BlockSpec((1, 2 * STEP, 2, HD // 2, PAIR), lambda i: (i // per_half, i % per_half, 0, 0, 0))
    params = pltpu.CompilerParams(vmem_limit_bytes=VMEM_LIMIT, dimension_semantics=("arbitrary",))
    like = jax.ShapeDtypeStruct((tokens, width), BF16)
    wide = jax.ShapeDtypeStruct((tokens, width), F32)
    states_shape = jax.ShapeDtypeStruct((2, slots, 2, HD // 2, PAIR), BF16)
    half_shape = jax.ShapeDtypeStruct((slots, 2, HD // 2, PAIR), BF16)

    query, key, states = pl.pallas_call(
        states_kernel,
        grid=(steps,),
        in_specs=[rows] * 4 + [table] * 2,
        out_specs=[rows, rows, chunk],
        out_shape=[like, like, states_shape],
        compiler_params=params,
    )(query_rows, key_rows, value_rows, out_grad, cosine, sine)

    cores = lax.all_to_all(states, "core", 0, 0, tiled=True)
    chip = whole(pair_sum_kernel, half_shape, cores)
    over_z = lax.all_to_all(chip, "z", 0, 0, tiled=True)

    flops = 12 * 2 * SPAN**3 * pairs
    query_in, key_in, value_in = pl.pallas_call(
        block_kernel,
        grid=(steps,),
        in_specs=[rows] * 4,
        out_specs=[rows] * 3,
        out_shape=[wide] * 3,
        compiler_params=params,
        cost_estimate=pl.CostEstimate(flops=flops, bytes_accessed=5 * 2**20, transcendentals=0),
    )(query, key, value_rows, out_grad)

    group = whole(
        totals_kernel, jax.ShapeDtypeStruct((n_ctx, HD // 2, PAIR), F32), over_z
    )
    over_ctx = lax.all_to_all(group, "ctx", 0, 0, tiled=True)
    sums = whole(scan_kernel, half_shape, over_z, over_ctx)
    back = lax.all_to_all(sums, "z", 0, 0, tiled=True)
    spread = whole(spread_kernel, states_shape, back, cores)
    carried = lax.all_to_all(spread, "core", 0, 0, tiled=True)

    return pl.pallas_call(
        functools.partial(finish_kernel, factor),
        grid=(steps,),
        in_specs=[rows] * 3 + [table] * 2 + [chunk] + [rows] * 3,
        out_specs=[rows] * 3,
        out_shape=[like] * 3,
        compiler_params=params,
    )(key, value_rows, out_grad, cosine, sine, carried, query_in, key_in, value_in)


def solution(mesh):
    split = Mesh(
        mesh.devices.reshape(mesh.shape["ctx"], mesh.shape["sp"] // 2, 2), ("ctx", "z", "core")
    )
    tokens = ("ctx", "z", "core")
    return jax.shard_map(
        on_device,
        mesh=split,
        in_specs=(P(tokens, None),) * 4 + (P(tokens),),
        out_specs=(P(tokens, None),) * 3,
        check_vma=False,
    )
```

```python
import functools
import math

import jax
import jax.numpy as jnp
from jax import lax
from jax.experimental import pallas as pl
from jax.experimental.pallas import tpu as pltpu
from jax.sharding import Mesh, PartitionSpec as P

HD = 64
SPAN = 128
BASE = 500000.0
PAIR = 2 * HD
HALF = HD // 2
F32 = jnp.float32
BF16 = jnp.bfloat16
GROUP = 4
VMEM_LIMIT = 16 * 1024 * 1024

NT = (((1,), (1,)), ((), ()))
TN = (((0,), (0,)), ((), ()))
NN = (((1,), (0,)), ((), ()))


def dot(a, b, dims):
    return lax.dot_general(a, b, dims, preferred_element_type=F32)


def lanes(rows):
    return lax.broadcasted_iota(jnp.int32, (rows, PAIR), 1)


def swap_halves(x):
    first = (lanes(x.shape[0]) % HD) < HALF
    return jnp.where(first, pltpu.roll(x, PAIR - HALF, 1), pltpu.roll(x, HALF, 1))


def rotated(x, cosine, sine):
    x = x.astype(F32)
    return x * cosine + swap_halves(x) * sine


def by_head(x):
    first = lanes(x.shape[0]) < HD
    zero = jnp.zeros_like(x)
    return jnp.concatenate([jnp.where(first, x, zero), jnp.where(first, zero, x)], axis=0)


def pack_pair(m):
    first = lanes(HD) < HD
    return jnp.where(first, m[:HD], m[HD:])


def angle_tables(positions):
    lane = lanes(1) % HALF
    frequency = jnp.ones((1, PAIR), F32)
    for bit in range(HALF.bit_length() - 1):
        part = BASE ** (-(2.0**bit) / HALF)
        frequency = jnp.where((lane >> bit) % 2 == 1, frequency * part, frequency)
    tokens = positions.shape[1]
    angles = jnp.broadcast_to(positions.astype(F32), (tokens, tokens)).T * frequency
    sign = jnp.where(lanes(1) % HD < HALF, -1.0, 1.0)
    return jnp.cos(angles), jnp.sin(angles) * sign


def span(first, count=1):
    return pl.ds(pl.multiple_of(first * PAIR, PAIR), count * PAIR)


def states_kernel(
    pos_ref, q_in, k_in, v_in, g_in,
    qr_ref, kr_ref, v_ref, g_ref, cos_ref, sin_ref, theirs_ref, mine_ref,
    q_ref, k_ref, sems,
):
    pairs = q_ref.shape[1] // PAIR
    core = lax.axis_index("core")
    first = (1 - core) * (pairs // 2)
    sources = ((q_in, q_ref), (k_in, k_ref), (v_in, v_ref), (g_in, g_ref))

    def copies(group):
        at = span(lax.rem(first + group * GROUP, pairs), GROUP)
        return [
            pltpu.make_async_copy(src.at[:, at], dst.at[:, at], sems.at[group, i])
            for i, (src, dst) in enumerate(sources)
        ]

    for group in range(pairs // GROUP):
        for copy in copies(group):
            copy.start()
    cosine, sine = angle_tables(pos_ref[...])
    cos_ref[...] = cosine
    sin_ref[...] = sine
    for j in range(pairs):
        if j % GROUP == 0:
            for copy in copies(j // GROUP):
                copy.wait()
        at = span(lax.rem(first + j, pairs))
        q = rotated(q_ref[:, at], cosine, sine).astype(BF16)
        k = rotated(k_ref[:, at], cosine, sine).astype(BF16)
        qr_ref[:, at] = q
        kr_ref[:, at] = k
        state = pack_pair(dot(k, v_ref[:, at], TN))
        grad = pack_pair(dot(q, g_ref[:, at], TN))
        out, slot = (theirs_ref, 2 * j) if j < pairs // 2 else (mine_ref, 2 * j - pairs)
        for r in range(2):
            rows = slice(HALF * r, HALF * (r + 1))
            out[slot + r, 0] = state[rows].astype(out.dtype)
            out[slot + r, 1] = grad[rows].astype(out.dtype)


def block_kernel(q_ref, k_ref, v_ref, g_ref, qo_ref, ko_ref, vo_ref):
    row = lax.broadcasted_iota(jnp.int32, (SPAN, 2 * SPAN), 0)
    col = lax.broadcasted_iota(jnp.int32, (SPAN, 2 * SPAN), 1) % SPAN
    lower = row >= col
    upper = row <= col
    for p in range(q_ref.shape[1] // PAIR):
        at = slice(p * PAIR, (p + 1) * PAIR)
        q, k, v, g = q_ref[:, at], k_ref[:, at], v_ref[:, at], g_ref[:, at]
        q2, k2, v2, g2 = by_head(q), by_head(k), by_head(v), by_head(g)
        w = jnp.where(lower, dot(g, v2, NT), 0.0).astype(BF16)
        wt = jnp.where(upper, dot(v, g2, NT), 0.0).astype(BF16)
        st = jnp.where(upper, dot(k, q2, NT), 0.0).astype(BF16)
        qo_ref[:, at] = dot(w, k2, NN)
        ko_ref[:, at] = dot(wt, q2, NN)
        vo_ref[:, at] = dot(st, g2, NN)


def chip_kernel(mine_ref, theirs_ref, out_ref):
    other = 1 - lax.axis_index("core")
    for z in range(out_ref.shape[0]):
        out_ref[z] = (mine_ref[z] + theirs_ref[other, z].astype(F32)).astype(BF16)


def totals_kernel(zr_ref, out_ref):
    state = zr_ref[0, 0].astype(F32)
    grad = zr_ref[0, 1].astype(F32)
    for z in range(1, zr_ref.shape[0]):
        state += zr_ref[z, 0].astype(F32)
        grad += zr_ref[z, 1].astype(F32)
    me = lax.axis_index("ctx")
    for j in range(out_ref.shape[0]):
        out_ref[j] = jnp.where(j > me, state, grad)


def scan_kernel(zr_ref, cx_ref, out_ref):
    me = lax.axis_index("ctx")
    state = jnp.zeros(cx_ref.shape[1:], F32)
    grad = jnp.zeros(cx_ref.shape[1:], F32)
    for j in range(cx_ref.shape[0]):
        state += jnp.where(j < me, cx_ref[j], 0.0)
        grad += jnp.where(j > me, cx_ref[j], 0.0)
    count = zr_ref.shape[0]
    for z in range(count):
        out_ref[z, 0] = state.astype(BF16)
        state += zr_ref[z, 0].astype(F32)
    for z in reversed(range(count)):
        out_ref[z, 1] = grad.astype(BF16)
        grad += zr_ref[z, 1].astype(F32)


def send_kernel(zb_ref, mine_ref, out_ref):
    core = lax.axis_index("core")
    for z in range(zb_ref.shape[0]):
        out_ref[z, 0] = (zb_ref[z, 0].astype(F32) + jnp.where(core == 0, mine_ref[z, 0], 0.0)).astype(BF16)
        out_ref[z, 1] = (zb_ref[z, 1].astype(F32) + jnp.where(core == 1, mine_ref[z, 1], 0.0)).astype(BF16)


def finish_kernel(
    factor, k_ref, v_ref, g_ref, cos_ref, sin_ref, zb_ref, theirs_ref, sent_ref, qi_ref, ki_ref, vi_ref,
    q_out, k_out, v_out, qo_ref, ko_ref, vo_ref, sems,
):
    pairs = k_ref.shape[1] // PAIR
    core = lax.axis_index("core")
    other = 1 - core
    first = core * (pairs // 2)
    cosine, sine = cos_ref[...], -sin_ref[...]
    results = ((qo_ref, q_out), (ko_ref, k_out), (vo_ref, v_out))
    copies = []

    def carried(slot, kind):
        count = zb_ref.shape[0]
        if slot >= count:
            return sent_ref[other, slot - count, kind]
        near = theirs_ref[other, slot, kind].astype(F32)
        return (zb_ref[slot, kind].astype(F32) + jnp.where(core == 1 - kind, near, 0.0)).astype(BF16)

    for j in range(pairs):
        at = span(lax.rem(first + j, pairs))
        k, v, g = k_ref[:, at], v_ref[:, at], g_ref[:, at]
        before = by_head(jnp.concatenate([carried(2 * j, 0), carried(2 * j + 1, 0)], axis=0))
        after = by_head(jnp.concatenate([carried(2 * j, 1), carried(2 * j + 1, 1)], axis=0))
        qo = (factor * (qi_ref[:, at] + dot(g, before, NT))).astype(BF16)
        ko = (factor * (ki_ref[:, at] + dot(v, after, NT))).astype(BF16)
        vo_ref[:, at] = (factor * (vi_ref[:, at] + dot(k, after, NN))).astype(BF16)
        qo_ref[:, at] = rotated(qo, cosine, sine).astype(BF16)
        ko_ref[:, at] = rotated(ko, cosine, sine).astype(BF16)
        if j % GROUP == GROUP - 1:
            group = j // GROUP
            done = span(lax.rem(first + group * GROUP, pairs), GROUP)
            for i, (src, dst) in enumerate(results):
                copies.append(pltpu.make_async_copy(src.at[:, done], dst.at[:, done], sems.at[group, i]))
                copies[-1].start()
    for copy in copies:
        copy.wait()


VMEM = pl.BlockSpec(memory_space=pltpu.VMEM)
HBM = pl.BlockSpec(memory_space=pltpu.HBM)


def call(kernel, out_shape, *args, out_specs=VMEM, in_specs=None, scratch=(), flops=0):
    in_specs = in_specs or [VMEM] * len(args)
    args = [pltpu.with_memory_space_constraint(x, spec.memory_space) for x, spec in zip(args, in_specs)]
    placed = jax.tree.map(lambda spec, x: spec.memory_space(x.shape, x.dtype), out_specs, out_shape)
    return pl.pallas_call(
        kernel,
        out_shape=placed,
        in_specs=in_specs,
        out_specs=out_specs,
        scratch_shapes=scratch,
        compiler_params=pltpu.CompilerParams(vmem_limit_bytes=VMEM_LIMIT),
        cost_estimate=pl.CostEstimate(flops=flops, bytes_accessed=2**20, transcendentals=0),
    )(*args)


def on_device(query_rows, key_rows, value_rows, out_grad, positions):
    tokens, width = query_rows.shape
    n_ctx, n_z = lax.axis_size("ctx"), lax.axis_size("z")
    seq_total = tokens * n_ctx * n_z * lax.axis_size("core")
    factor = 1.0 / math.sqrt(HD * seq_total)
    pairs = width // PAIR
    groups = pairs // GROUP
    like = jax.ShapeDtypeStruct((tokens, width), BF16)
    wide = jax.ShapeDtypeStruct((tokens, width), F32)
    table = jax.ShapeDtypeStruct((tokens, PAIR), F32)
    half_low = jax.ShapeDtypeStruct((pairs, 2, HALF, PAIR), BF16)
    half_wide = jax.ShapeDtypeStruct((pairs, 2, HALF, PAIR), F32)

    query, key, value, grad, cosine, sine, theirs, mine = call(
        states_kernel,
        [like] * 4 + [table] * 2 + [half_low, half_wide],
        positions.reshape(1, tokens), query_rows, key_rows, value_rows, out_grad,
        in_specs=[VMEM] + [HBM] * 4,
        out_specs=[VMEM] * 8,
        scratch=[pltpu.VMEM((tokens, width), BF16)] * 2 + [pltpu.SemaphoreType.DMA((groups, 4))],
    )
    theirs = lax.all_gather(theirs, "core")
    chip = call(chip_kernel, half_low, mine, theirs)
    over_z = lax.all_to_all(chip, "z", 0, 0, tiled=True)

    query_in, key_in, value_in = call(
        block_kernel, [wide] * 3, query, key, value, grad, out_specs=[VMEM] * 3, flops=24 * SPAN**3 * pairs
    )

    group = call(totals_kernel, jax.ShapeDtypeStruct((n_ctx, HALF, PAIR), F32), over_z)
    over_ctx = lax.all_to_all(group, "ctx", 0, 0, tiled=True)
    sums = call(scan_kernel, half_low, over_z, over_ctx)
    back = lax.all_to_all(sums, "z", 0, 0, tiled=True)
    sent = lax.all_gather(call(send_kernel, half_low, back, mine), "core")

    return call(
        functools.partial(finish_kernel, factor),
        [like] * 3,
        key, value, grad, cosine, sine, back, theirs, sent, query_in, key_in, value_in,
        out_specs=[HBM] * 3,
        scratch=[pltpu.VMEM((tokens, width), BF16)] * 3 + [pltpu.SemaphoreType.DMA((groups, 3))],
    )


def solution(mesh):
    split = Mesh(
        mesh.devices.reshape(mesh.shape["ctx"], mesh.shape["sp"] // 2, 2), ("ctx", "z", "core")
    )
    tokens = ("ctx", "z", "core")
    return jax.shard_map(
        on_device,
        mesh=split,
        in_specs=(P(tokens, None),) * 4 + (P(tokens),),
        out_specs=(P(tokens, None),) * 3,
        check_vma=False,
    )
```

```python
import functools
import math

import jax
import jax.numpy as jnp
from jax import lax
from jax.experimental import pallas as pl
from jax.experimental.pallas import tpu as pltpu
from jax.sharding import Mesh, PartitionSpec as P

HD = 64
SPAN = 128
BASE = 500000.0
PAIR = 2 * HD
HALF = HD // 2
F32 = jnp.float32
BF16 = jnp.bfloat16
GROUP = 4
VMEM_LIMIT = 16 * 1024 * 1024

NT = (((1,), (1,)), ((), ()))
TN = (((0,), (0,)), ((), ()))
NN = (((1,), (0,)), ((), ()))


def dot(a, b, dims):
    return lax.dot_general(a, b, dims, preferred_element_type=F32)


def lanes(rows):
    return lax.broadcasted_iota(jnp.int32, (rows, PAIR), 1)


def swap_halves(x):
    first = (lanes(x.shape[0]) % HD) < HALF
    return jnp.where(first, pltpu.roll(x, PAIR - HALF, 1), pltpu.roll(x, HALF, 1))


def rotated(x, cosine, sine):
    x = x.astype(F32)
    return x * cosine + swap_halves(x) * sine


def by_head(x):
    first = lanes(x.shape[0]) < HD
    zero = jnp.zeros_like(x)
    return jnp.concatenate([jnp.where(first, x, zero), jnp.where(first, zero, x)], axis=0)


def pack_pair(m):
    first = lanes(HD) < HD
    return jnp.where(first, m[:HD], m[HD:])


def angle_tables(positions):
    lane = lanes(1) % HALF
    frequency = jnp.ones((1, PAIR), F32)
    for bit in range(HALF.bit_length() - 1):
        part = BASE ** (-(2.0**bit) / HALF)
        frequency = jnp.where((lane >> bit) % 2 == 1, frequency * part, frequency)
    tokens = positions.shape[1]
    angles = jnp.broadcast_to(positions.astype(F32), (tokens, tokens)).T * frequency
    sign = jnp.where(lanes(1) % HD < HALF, -1.0, 1.0)
    return jnp.cos(angles), jnp.sin(angles) * sign


def span(first, count=1):
    return pl.ds(pl.multiple_of(first * PAIR, PAIR), count * PAIR)


def loads(sources, sems, first):
    pairs = sources[0][0].shape[1] // PAIR
    groups = []
    for group in range(pairs // GROUP):
        at = span(lax.rem(first + group * GROUP, pairs), GROUP)
        groups.append(
            [
                pltpu.make_async_copy(src.at[:, at], dst.at[:, at], sems.at[group, i])
                for i, (src, dst) in enumerate(sources)
            ]
        )
    for copies in groups:
        for copy in copies:
            copy.start()
    return groups


def store(results, sems, first, group):
    pairs = results[0][0].shape[1] // PAIR
    at = span(lax.rem(first + group * GROUP, pairs), GROUP)
    copies = [
        pltpu.make_async_copy(src.at[:, at], dst.at[:, at], sems.at[group, i])
        for i, (src, dst) in enumerate(results)
    ]
    for copy in copies:
        copy.start()
    return copies


def states_kernel(
    pos_in, q_in, k_in, v_in, g_in,
    cos_ref, sin_ref, theirs_ref, mine_ref,
    pos_ref, q_ref, k_ref, v_ref, g_ref, sems, pos_sem,
):
    pairs = q_ref.shape[1] // PAIR
    core = lax.axis_index("core")
    first = (1 - core) * (pairs // 2)
    pos_copy = pltpu.make_async_copy(pos_in, pos_ref, pos_sem)
    pos_copy.start()
    groups = loads(((q_in, q_ref), (k_in, k_ref), (v_in, v_ref), (g_in, g_ref)), sems, first)
    pos_copy.wait()
    cosine, sine = angle_tables(pos_ref[...])
    cos_ref[...] = cosine
    sin_ref[...] = sine
    for j in range(pairs):
        if j % GROUP == 0:
            for copy in groups[j // GROUP]:
                copy.wait()
        at = span(lax.rem(first + j, pairs))
        q = rotated(q_ref[:, at], cosine, sine).astype(BF16)
        k = rotated(k_ref[:, at], cosine, sine).astype(BF16)
        state = pack_pair(dot(k, v_ref[:, at], TN))
        grad = pack_pair(dot(q, g_ref[:, at], TN))
        out, slot = (theirs_ref, 2 * j) if j < pairs // 2 else (mine_ref, 2 * j - pairs)
        for r in range(2):
            rows = slice(HALF * r, HALF * (r + 1))
            out[slot + r, 0] = state[rows].astype(out.dtype)
            out[slot + r, 1] = grad[rows].astype(out.dtype)


def block_kernel(
    q_in, k_in, v_in, g_in, cos_ref, sin_ref, kr_out, q_out, k_out, v_out,
    q_ref, k_ref, v_ref, g_ref, kr_ref, qo_ref, ko_ref, vo_ref, sems, out_sems,
):
    groups = loads(((q_in, q_ref), (k_in, k_ref), (v_in, v_ref), (g_in, g_ref)), sems, 0)
    results = ((kr_ref, kr_out), (qo_ref, q_out), (ko_ref, k_out), (vo_ref, v_out))
    cosine, sine = cos_ref[...], sin_ref[...]
    row = lax.broadcasted_iota(jnp.int32, (SPAN, 2 * SPAN), 0)
    col = lax.broadcasted_iota(jnp.int32, (SPAN, 2 * SPAN), 1) % SPAN
    lower = row >= col
    upper = row <= col
    stores = []
    for p in range(q_ref.shape[1] // PAIR):
        if p % GROUP == 0:
            for copy in groups[p // GROUP]:
                copy.wait()
        at = slice(p * PAIR, (p + 1) * PAIR)
        q = rotated(q_ref[:, at], cosine, sine).astype(BF16)
        k = rotated(k_ref[:, at], cosine, sine).astype(BF16)
        v, g = v_ref[:, at], g_ref[:, at]
        kr_ref[:, at] = k
        q2, k2, v2, g2 = by_head(q), by_head(k), by_head(v), by_head(g)
        w = jnp.where(lower, dot(g, v2, NT), 0.0).astype(BF16)
        wt = jnp.where(upper, dot(v, g2, NT), 0.0).astype(BF16)
        st = jnp.where(upper, dot(k, q2, NT), 0.0).astype(BF16)
        qo_ref[:, at] = dot(w, k2, NN)
        ko_ref[:, at] = dot(wt, q2, NN)
        vo_ref[:, at] = dot(st, g2, NN)
        if p % GROUP == GROUP - 1:
            stores += store(results, out_sems, 0, p // GROUP)
    for copy in stores:
        copy.wait()


def chip_kernel(mine_ref, theirs_ref, out_ref):
    other = 1 - lax.axis_index("core")
    for z in range(out_ref.shape[0]):
        out_ref[z] = (mine_ref[z] + theirs_ref[other, z].astype(F32)).astype(BF16)


def totals_kernel(zr_ref, ready_in, out_ref):
    del ready_in
    state = zr_ref[0, 0].astype(F32)
    grad = zr_ref[0, 1].astype(F32)
    for z in range(1, zr_ref.shape[0]):
        state += zr_ref[z, 0].astype(F32)
        grad += zr_ref[z, 1].astype(F32)
    me = lax.axis_index("ctx")
    for j in range(out_ref.shape[0]):
        out_ref[j] = jnp.where(j > me, state, grad)


def scan_kernel(zr_ref, cx_ref, out_ref):
    me = lax.axis_index("ctx")
    state = jnp.zeros(cx_ref.shape[1:], F32)
    grad = jnp.zeros(cx_ref.shape[1:], F32)
    for j in range(cx_ref.shape[0]):
        state += jnp.where(j < me, cx_ref[j], 0.0)
        grad += jnp.where(j > me, cx_ref[j], 0.0)
    count = zr_ref.shape[0]
    for z in range(count):
        out_ref[z, 0] = state.astype(BF16)
        state += zr_ref[z, 0].astype(F32)
    for z in reversed(range(count)):
        out_ref[z, 1] = grad.astype(BF16)
        grad += zr_ref[z, 1].astype(F32)


def send_kernel(zb_ref, mine_ref, out_ref):
    core = lax.axis_index("core")
    for z in range(zb_ref.shape[0]):
        out_ref[z, 0] = (zb_ref[z, 0].astype(F32) + jnp.where(core == 0, mine_ref[z, 0], 0.0)).astype(BF16)
        out_ref[z, 1] = (zb_ref[z, 1].astype(F32) + jnp.where(core == 1, mine_ref[z, 1], 0.0)).astype(BF16)


def finish_kernel(
    factor, k_ref, v_ref, g_ref, qi_ref, ki_ref, vi_ref, cos_ref, sin_ref, zb_ref, theirs_ref, sent_ref,
    q_out, k_out, v_out, qo_ref, ko_ref, vo_ref, out_sems,
):
    pairs = k_ref.shape[1] // PAIR
    core = lax.axis_index("core")
    other = 1 - core
    first = core * (pairs // 2)
    results = ((qo_ref, q_out), (ko_ref, k_out), (vo_ref, v_out))
    cosine, sine = cos_ref[...], -sin_ref[...]
    stores = []

    def carried(slot, kind):
        count = zb_ref.shape[0]
        if slot >= count:
            return sent_ref[other, slot - count, kind]
        near = theirs_ref[other, slot, kind].astype(F32)
        return (zb_ref[slot, kind].astype(F32) + jnp.where(core == 1 - kind, near, 0.0)).astype(BF16)

    for j in range(pairs):
        at = span(lax.rem(first + j, pairs))
        k, v, g = k_ref[:, at], v_ref[:, at], g_ref[:, at]
        before = by_head(jnp.concatenate([carried(2 * j, 0), carried(2 * j + 1, 0)], axis=0))
        after = by_head(jnp.concatenate([carried(2 * j, 1), carried(2 * j + 1, 1)], axis=0))
        qo = (factor * (qi_ref[:, at] + dot(g, before, NT))).astype(BF16)
        ko = (factor * (ki_ref[:, at] + dot(v, after, NT))).astype(BF16)
        vo_ref[:, at] = (factor * (vi_ref[:, at] + dot(k, after, NN))).astype(BF16)
        qo_ref[:, at] = rotated(qo, cosine, sine).astype(BF16)
        ko_ref[:, at] = rotated(ko, cosine, sine).astype(BF16)
        if j % GROUP == GROUP - 1:
            stores += store(results, out_sems, first, j // GROUP)
    for copy in stores:
        copy.wait()


VMEM = pl.BlockSpec(memory_space=pltpu.VMEM)
HBM = pl.BlockSpec(memory_space=pltpu.HBM)


def call(kernel, out_shape, *args, out_specs=VMEM, in_specs=None, scratch=(), flops=0):
    in_specs = in_specs or [VMEM] * len(args)
    args = [pltpu.with_memory_space_constraint(x, spec.memory_space) for x, spec in zip(args, in_specs)]
    placed = jax.tree.map(lambda spec, x: spec.memory_space(x.shape, x.dtype), out_specs, out_shape)
    return pl.pallas_call(
        kernel,
        out_shape=placed,
        in_specs=in_specs,
        out_specs=out_specs,
        scratch_shapes=scratch,
        compiler_params=pltpu.CompilerParams(vmem_limit_bytes=VMEM_LIMIT),
        cost_estimate=pl.CostEstimate(flops=flops, bytes_accessed=2**20, transcendentals=0),
    )(*args)


def on_device(query_rows, key_rows, value_rows, out_grad, positions):
    tokens, width = query_rows.shape
    n_ctx, n_z = lax.axis_size("ctx"), lax.axis_size("z")
    seq_total = tokens * n_ctx * n_z * lax.axis_size("core")
    factor = 1.0 / math.sqrt(HD * seq_total)
    pairs = width // PAIR
    groups = pairs // GROUP
    like = jax.ShapeDtypeStruct((tokens, width), BF16)
    wide = jax.ShapeDtypeStruct((tokens, width), F32)
    table = jax.ShapeDtypeStruct((tokens, PAIR), F32)
    half_low = jax.ShapeDtypeStruct((pairs, 2, HALF, PAIR), BF16)
    half_wide = jax.ShapeDtypeStruct((pairs, 2, HALF, PAIR), F32)

    low, high = pltpu.VMEM((tokens, width), BF16), pltpu.VMEM((tokens, width), F32)

    def sems(count):
        return pltpu.SemaphoreType.DMA((groups, count))

    cosine, sine, theirs, mine = call(
        states_kernel,
        [table] * 2 + [half_low, half_wide],
        positions.reshape(1, tokens), query_rows, key_rows, value_rows, out_grad,
        in_specs=[HBM] * 5,
        out_specs=[VMEM] * 4,
        scratch=[pltpu.VMEM((1, tokens), jnp.int32)] + [low] * 4 + [sems(4), pltpu.SemaphoreType.DMA],
    )
    theirs = lax.all_gather(theirs, "core")
    chip = call(chip_kernel, half_low, mine, theirs)
    over_z = lax.all_to_all(chip, "z", 0, 0, tiled=True)

    key, query_in, key_in, value_in = call(
        block_kernel,
        [like] + [wide] * 3,
        query_rows, key_rows, value_rows, out_grad, cosine, sine,
        in_specs=[HBM] * 4 + [VMEM] * 2,
        out_specs=[HBM] * 4,
        scratch=[low] * 5 + [high] * 3 + [sems(4), sems(4)],
        flops=24 * SPAN**3 * pairs,
    )

    group = call(
        totals_kernel, jax.ShapeDtypeStruct((n_ctx, HALF, PAIR), F32), over_z, query_in, in_specs=[VMEM, HBM]
    )
    over_ctx = lax.all_to_all(group, "ctx", 0, 0, tiled=True)
    sums = call(scan_kernel, half_low, over_z, over_ctx)
    back = lax.all_to_all(sums, "z", 0, 0, tiled=True)
    sent = lax.all_gather(call(send_kernel, half_low, back, mine), "core")

    return call(
        functools.partial(finish_kernel, factor),
        [like] * 3,
        key, value_rows, out_grad, query_in, key_in, value_in, cosine, sine, back, theirs, sent,
        out_specs=[HBM] * 3,
        scratch=[low] * 3 + [sems(3)],
    )


def solution(mesh):
    split = Mesh(
        mesh.devices.reshape(mesh.shape["ctx"], mesh.shape["sp"] // 2, 2), ("ctx", "z", "core")
    )
    tokens = ("ctx", "z", "core")
    return jax.shard_map(
        on_device,
        mesh=split,
        in_specs=(P(tokens, None),) * 4 + (P(tokens),),
        out_specs=(P(tokens, None),) * 3,
        check_vma=False,
    )
```

```python
import functools
import math

import jax
import jax.numpy as jnp
from jax import lax
from jax.experimental import pallas as pl
from jax.experimental.pallas import tpu as pltpu
from jax.sharding import Mesh, PartitionSpec as P

HD = 64
SPAN = 128
BASE = 500000.0
PAIR = 2 * HD
HALF = HD // 2
F32 = jnp.float32
BF16 = jnp.bfloat16
GROUP = 4
AGAIN = 8
VMEM_LIMIT = 16 * 1024 * 1024

NT = (((1,), (1,)), ((), ()))
TN = (((0,), (0,)), ((), ()))
NN = (((1,), (0,)), ((), ()))


def dot(a, b, dims):
    return lax.dot_general(a, b, dims, preferred_element_type=F32)


def lanes(rows):
    return lax.broadcasted_iota(jnp.int32, (rows, PAIR), 1)


def swap_halves(x):
    first = (lanes(x.shape[0]) % HD) < HALF
    return jnp.where(first, pltpu.roll(x, PAIR - HALF, 1), pltpu.roll(x, HALF, 1))


def swap_matrix():
    row = lax.broadcasted_iota(jnp.int32, (PAIR, PAIR), 0)
    lane = lanes(PAIR)
    source = jnp.where(lane % HD < HALF, lane + HALF, lane - HALF)
    return jnp.where(row == source, 1.0, 0.0).astype(BF16)


def rotated(x, cosine, sine):
    x = x.astype(F32)
    return x * cosine + swap_halves(x) * sine


def by_head(x):
    first = lanes(x.shape[0]) < HD
    zero = jnp.zeros_like(x)
    return jnp.concatenate([jnp.where(first, x, zero), jnp.where(first, zero, x)], axis=0)


def pack_pair(m):
    first = lanes(HD) < HD
    return jnp.where(first, m[:HD], m[HD:])


def angle_tables(positions):
    lane = lanes(1) % HALF
    frequency = jnp.ones((1, PAIR), F32)
    for bit in range(HALF.bit_length() - 1):
        part = BASE ** (-(2.0**bit) / HALF)
        frequency = jnp.where((lane >> bit) % 2 == 1, frequency * part, frequency)
    tokens = positions.shape[1]
    angles = jnp.broadcast_to(positions.astype(F32), (tokens, tokens)).T * frequency
    sign = jnp.where(lanes(1) % HD < HALF, -1.0, 1.0)
    return jnp.cos(angles), jnp.sin(angles) * sign


def span(first, count=1):
    return pl.ds(pl.multiple_of(first * PAIR, PAIR), count * PAIR)


def store(results, sems, first, group):
    pairs = results[0][0].shape[1] // PAIR
    at = span(lax.rem(first + group * GROUP, pairs), GROUP)
    copies = [
        pltpu.make_async_copy(src.at[:, at], dst.at[:, at], sems.at[group, i])
        for i, (src, dst) in enumerate(results)
    ]
    for copy in copies:
        copy.start()
    return copies


def states_kernel(
    pos_in, q_in, k_in, v_in, g_in,
    qr_ref, kr_ref, v_ref, g_ref, cos_ref, sin_ref, theirs_ref, mine_ref,
    pos_ref, q_ref, k_ref, sems, pos_sem,
):
    pairs = q_ref.shape[1] // PAIR
    first = (1 - lax.axis_index("core")) * (pairs // 2)
    pos_copy = pltpu.make_async_copy(pos_in, pos_ref, pos_sem)
    pos_copy.start()
    arrays = ((q_in, q_ref), (g_in, g_ref), (k_in, k_ref), (v_in, v_ref))
    copies = [pltpu.make_async_copy(src, dst, sems.at[i]) for i, (src, dst) in enumerate(arrays)]
    for copy in copies:
        copy.start()
    pos_copy.wait()
    cosine, sine = angle_tables(pos_ref[...])
    cos_ref[...] = cosine
    sin_ref[...] = sine
    swap = swap_matrix()
    for kind, left, turned, right in ((1, q_ref, qr_ref, g_ref), (0, k_ref, kr_ref, v_ref)):
        copies[2 - 2 * kind].wait()
        copies[3 - 2 * kind].wait()
        for j in range(pairs):
            at = span(lax.rem(first + j, pairs))
            x = left[:, at]
            x = (x.astype(F32) * cosine + dot(x, swap, NN) * sine).astype(BF16)
            turned[:, at] = x
            state = pack_pair(dot(x, right[:, at], TN))
            out, slot = (theirs_ref, 2 * j) if j < pairs // 2 else (mine_ref, 2 * j - pairs)
            for r in range(2):
                out[slot + r, kind] = state[HALF * r : HALF * (r + 1)].astype(out.dtype)


def block_products(q_ref, k_ref, v_ref, g_ref, qo_ref, ko_ref, vo_ref, again=0):
    row = lax.broadcasted_iota(jnp.int32, (SPAN, 2 * SPAN), 0)
    col = lax.broadcasted_iota(jnp.int32, (SPAN, 2 * SPAN), 1) % SPAN
    lower = row >= col
    upper = row <= col
    pairs = q_ref.shape[1] // PAIR
    for p in [*range(again), *range(pairs)]:
        at = slice(p * PAIR, (p + 1) * PAIR)
        q, k, v, g = q_ref[:, at], k_ref[:, at], v_ref[:, at], g_ref[:, at]
        q2, k2, v2, g2 = by_head(q), by_head(k), by_head(v), by_head(g)
        w = jnp.where(lower, dot(g, v2, NT), 0.0).astype(BF16)
        wt = jnp.where(upper, dot(v, g2, NT), 0.0).astype(BF16)
        st = jnp.where(upper, dot(k, q2, NT), 0.0).astype(BF16)
        qo_ref[:, at] = dot(w, k2, NN)
        ko_ref[:, at] = dot(wt, q2, NN)
        vo_ref[:, at] = dot(st, g2, NN)


def chip_kernel(mine_ref, theirs_ref, q_ref, k_ref, v_ref, g_ref, out_ref, qo_ref, ko_ref, vo_ref):
    core = lax.axis_index("core")
    for z in range(out_ref.shape[0]):
        out_ref[z] = (mine_ref[z] + theirs_ref[1 - core, z].astype(F32)).astype(BF16)

    @pl.when(core == 0)
    def _():
        block_products(q_ref, k_ref, v_ref, g_ref, qo_ref, ko_ref, vo_ref, AGAIN)


def totals_kernel(zr_ref, out_ref):
    state = zr_ref[0, 0].astype(F32)
    grad = zr_ref[0, 1].astype(F32)
    for z in range(1, zr_ref.shape[0]):
        state += zr_ref[z, 0].astype(F32)
        grad += zr_ref[z, 1].astype(F32)
    me = lax.axis_index("ctx")
    for j in range(out_ref.shape[0]):
        out_ref[j] = jnp.where(j > me, state, grad)


def scan_kernel(zr_ref, cx_ref, out_ref):
    me = lax.axis_index("ctx")
    state = jnp.zeros(cx_ref.shape[1:], F32)
    grad = jnp.zeros(cx_ref.shape[1:], F32)
    for j in range(cx_ref.shape[0]):
        state += jnp.where(j < me, cx_ref[j], 0.0)
        grad += jnp.where(j > me, cx_ref[j], 0.0)
    count = zr_ref.shape[0]
    for z in range(count):
        out_ref[z, 0] = state.astype(BF16)
        state += zr_ref[z, 0].astype(F32)
    for z in reversed(range(count)):
        out_ref[z, 1] = grad.astype(BF16)
        grad += zr_ref[z, 1].astype(F32)


def send_kernel(
    zb_ref, mine_ref, q_ref, k_ref, v_ref, g_ref, qi_ref, ki_ref, vi_ref, out_ref, qo_ref, ko_ref, vo_ref
):
    del qi_ref, ki_ref, vi_ref
    core = lax.axis_index("core")
    for z in range(zb_ref.shape[0]):
        out_ref[z, 0] = (zb_ref[z, 0].astype(F32) + jnp.where(core == 0, mine_ref[z, 0], 0.0)).astype(BF16)
        out_ref[z, 1] = (zb_ref[z, 1].astype(F32) + jnp.where(core == 1, mine_ref[z, 1], 0.0)).astype(BF16)

    @pl.when(core == 1)
    def _():
        block_products(q_ref, k_ref, v_ref, g_ref, qo_ref, ko_ref, vo_ref)


def finish_kernel(
    factor, k_ref, v_ref, g_ref, qi_ref, ki_ref, vi_ref, cos_ref, sin_ref, zb_ref, theirs_ref, sent_ref,
    q_out, k_out, v_out, qo_ref, ko_ref, vo_ref, out_sems,
):
    pairs = k_ref.shape[1] // PAIR
    core = lax.axis_index("core")
    other = 1 - core
    first = core * (pairs // 2)
    results = ((qo_ref, q_out), (ko_ref, k_out), (vo_ref, v_out))
    cosine, sine = cos_ref[...], -sin_ref[...]
    stores = []

    def carried(slot, kind):
        count = zb_ref.shape[0]
        if slot >= count:
            return sent_ref[other, slot - count, kind]
        near = theirs_ref[other, slot, kind].astype(F32)
        return (zb_ref[slot, kind].astype(F32) + jnp.where(core == 1 - kind, near, 0.0)).astype(BF16)

    for j in range(pairs):
        at = span(lax.rem(first + j, pairs))
        k, v, g = k_ref[:, at], v_ref[:, at], g_ref[:, at]
        before = by_head(jnp.concatenate([carried(2 * j, 0), carried(2 * j + 1, 0)], axis=0))
        after = by_head(jnp.concatenate([carried(2 * j, 1), carried(2 * j + 1, 1)], axis=0))
        qo = (factor * (qi_ref[:, at] + dot(g, before, NT))).astype(BF16)
        ko = (factor * (ki_ref[:, at] + dot(v, after, NT))).astype(BF16)
        vo_ref[:, at] = (factor * (vi_ref[:, at] + dot(k, after, NN))).astype(BF16)
        qo_ref[:, at] = rotated(qo, cosine, sine).astype(BF16)
        ko_ref[:, at] = rotated(ko, cosine, sine).astype(BF16)
        if j % GROUP == GROUP - 1:
            stores += store(results, out_sems, first, j // GROUP)
    for copy in stores:
        copy.wait()


VMEM = pl.BlockSpec(memory_space=pltpu.VMEM)
HBM = pl.BlockSpec(memory_space=pltpu.HBM)


def call(kernel, out_shape, *args, out_specs=VMEM, in_specs=None, scratch=(), aliases=None):
    in_specs = in_specs or [VMEM] * len(args)
    args = [pltpu.with_memory_space_constraint(x, spec.memory_space) for x, spec in zip(args, in_specs)]
    placed = jax.tree.map(lambda spec, x: spec.memory_space(x.shape, x.dtype), out_specs, out_shape)
    return pl.pallas_call(
        kernel,
        out_shape=placed,
        in_specs=in_specs,
        out_specs=out_specs,
        scratch_shapes=scratch,
        compiler_params=pltpu.CompilerParams(vmem_limit_bytes=VMEM_LIMIT),
        input_output_aliases=aliases or {},
    )(*args)


def on_device(query_rows, key_rows, value_rows, out_grad, positions):
    tokens, width = query_rows.shape
    n_ctx, n_z = lax.axis_size("ctx"), lax.axis_size("z")
    seq_total = tokens * n_ctx * n_z * lax.axis_size("core")
    factor = 1.0 / math.sqrt(HD * seq_total)
    pairs = width // PAIR
    groups = pairs // GROUP
    like = jax.ShapeDtypeStruct((tokens, width), BF16)
    wide = jax.ShapeDtypeStruct((tokens, width), F32)
    table = jax.ShapeDtypeStruct((tokens, PAIR), F32)
    half_low = jax.ShapeDtypeStruct((pairs, 2, HALF, PAIR), BF16)
    half_wide = jax.ShapeDtypeStruct((pairs, 2, HALF, PAIR), F32)

    query, key, value, grad, cosine, sine, theirs, mine = call(
        states_kernel,
        [like] * 4 + [table] * 2 + [half_low, half_wide],
        positions.reshape(1, tokens), query_rows, key_rows, value_rows, out_grad,
        in_specs=[HBM] * 5,
        out_specs=[VMEM] * 8,
        scratch=[
            pltpu.VMEM((1, tokens), jnp.int32), pltpu.VMEM((tokens, width), BF16), pltpu.VMEM((tokens, width), BF16),
            pltpu.SemaphoreType.DMA((4,)), pltpu.SemaphoreType.DMA,
        ],
    )
    rows = (query, key, value, grad)
    theirs = lax.all_gather(theirs, "core")
    chip, *inner = call(chip_kernel, [half_low] + [wide] * 3, mine, theirs, *rows, out_specs=[VMEM] * 4)
    over_z = lax.all_to_all(chip, "z", 0, 0, tiled=True)
    group = call(totals_kernel, jax.ShapeDtypeStruct((n_ctx, HALF, PAIR), F32), over_z)
    over_ctx = lax.all_to_all(group, "ctx", 0, 0, tiled=True)
    sums = call(scan_kernel, half_low, over_z, over_ctx)
    back = lax.all_to_all(sums, "z", 0, 0, tiled=True)
    send, *inner = call(
        send_kernel,
        [half_low] + [wide] * 3,
        back, mine, *rows, *inner,
        out_specs=[VMEM] * 4,
        aliases={6: 1, 7: 2, 8: 3},
    )
    sent = lax.all_gather(send, "core")
    return call(
        functools.partial(finish_kernel, factor),
        [like] * 3,
        key, value, grad, *inner, cosine, sine, back, theirs, sent,
        out_specs=[HBM] * 3,
        scratch=[pltpu.VMEM((tokens, width), BF16)] * 3 + [pltpu.SemaphoreType.DMA((groups, 3))],
    )


def solution(mesh):
    split = Mesh(
        mesh.devices.reshape(mesh.shape["ctx"], mesh.shape["sp"] // 2, 2), ("ctx", "z", "core")
    )
    tokens = ("ctx", "z", "core")
    return jax.shard_map(
        on_device,
        mesh=split,
        in_specs=(P(tokens, None),) * 4 + (P(tokens),),
        out_specs=(P(tokens, None),) * 3,
        check_vma=False,
    )
```

```python
import functools
import math

import jax
import jax.numpy as jnp
from jax import lax
from jax.experimental import pallas as pl
from jax.experimental.pallas import tpu as pltpu
from jax.sharding import Mesh, PartitionSpec as P

HD = 64
SPAN = 128
BASE = 500000.0
PAIR = 2 * HD
HALF = HD // 2
F32 = jnp.float32
BF16 = jnp.bfloat16
GROUP = 4
VMEM_LIMIT = 16 * 1024 * 1024

NT = (((1,), (1,)), ((), ()))
TN = (((0,), (0,)), ((), ()))
NN = (((1,), (0,)), ((), ()))


def dot(a, b, dims):
    return lax.dot_general(a, b, dims, preferred_element_type=F32)


def lanes(rows):
    return lax.broadcasted_iota(jnp.int32, (rows, PAIR), 1)


def swap_halves(x):
    first = (lanes(x.shape[0]) % HD) < HALF
    return jnp.where(first, pltpu.roll(x, PAIR - HALF, 1), pltpu.roll(x, HALF, 1))


def swap_matrix():
    row = lax.broadcasted_iota(jnp.int32, (PAIR, PAIR), 0)
    lane = lanes(PAIR)
    source = jnp.where(lane % HD < HALF, lane + HALF, lane - HALF)
    return jnp.where(row == source, 1.0, 0.0).astype(BF16)


def rotated(x, cosine, sine):
    return x.astype(F32) * cosine + swap_halves(x).astype(F32) * sine


def by_head(x):
    first = lanes(x.shape[0]) < HD
    zero = jnp.zeros_like(x)
    return jnp.concatenate([jnp.where(first, x, zero), jnp.where(first, zero, x)], axis=0)


def pack_pair(m):
    first = lanes(HD) < HD
    return jnp.where(first, m[:HD], m[HD:])


def angle_tables(positions):
    index = lax.broadcasted_iota(jnp.int32, (HALF, positions.shape[1]), 0)
    frequency = jnp.ones(index.shape, F32)
    for bit in range(HALF.bit_length() - 1):
        part = BASE ** (-(2.0**bit) / HALF)
        frequency = jnp.where((index >> bit) % 2 == 1, frequency * part, frequency)
    angles = positions.astype(F32) * frequency
    cosine, sine = jnp.cos(angles), jnp.sin(angles)
    return (
        jnp.concatenate([cosine, cosine, cosine, cosine], axis=0).T,
        jnp.concatenate([-sine, sine, -sine, sine], axis=0).T,
    )


def span(first, count=1):
    return pl.ds(pl.multiple_of(first * PAIR, PAIR), count * PAIR)


def store(results, sems, first, group):
    pairs = results[0][0].shape[1] // PAIR
    at = span(lax.rem(first + group * GROUP, pairs), GROUP)
    copies = [
        pltpu.make_async_copy(src.at[:, at], dst.at[:, at], sems.at[group, i])
        for i, (src, dst) in enumerate(results)
    ]
    for copy in copies:
        copy.start()
    return copies


def states_kernel(
    pos_in, q_in, k_in, v_in, g_in,
    cos_ref, sin_ref, theirs_ref, mine_ref,
    pos_ref, q_ref, k_ref, v_ref, g_ref, sems, pos_sem,
):
    pairs = q_ref.shape[1] // PAIR
    first = (1 - lax.axis_index("core")) * (pairs // 2)
    pos_copy = pltpu.make_async_copy(pos_in, pos_ref, pos_sem)
    pos_copy.start()
    arrays = ((q_in, q_ref), (g_in, g_ref), (k_in, k_ref), (v_in, v_ref))
    copies = [pltpu.make_async_copy(src, dst, sems.at[i]) for i, (src, dst) in enumerate(arrays)]
    for copy in copies:
        copy.start()
    pos_copy.wait()
    cosine, sine = angle_tables(pos_ref[...])
    cos_ref[...] = cosine
    sin_ref[...] = sine
    swap = swap_matrix()
    for kind, left, right in ((1, q_ref, g_ref), (0, k_ref, v_ref)):
        copies[2 - 2 * kind].wait()
        copies[3 - 2 * kind].wait()
        for j in range(pairs):
            at = span(lax.rem(first + j, pairs))
            x = left[:, at]
            x = (x.astype(F32) * cosine + dot(x, swap, NN) * sine).astype(BF16)
            state = pack_pair(dot(x, right[:, at], TN))
            out, slot = (theirs_ref, 2 * j) if j < pairs // 2 else (mine_ref, 2 * j - pairs)
            for r in range(2):
                out[slot + r, kind] = state[HALF * r : HALF * (r + 1)].astype(out.dtype)


def block_products(
    q_in, k_in, v_in, g_in, cos_ref, sin_ref, kr_ref, v_ref, g_ref, qo_ref, ko_ref, vo_ref, q_ref, k_ref, sems
):
    pairs = q_ref.shape[1] // PAIR
    arrays = ((q_in, q_ref), (k_in, k_ref), (v_in, v_ref), (g_in, g_ref))
    copies = []
    for group in range(pairs // GROUP):
        at = slice(group * GROUP * PAIR, (group + 1) * GROUP * PAIR)
        copies.append(
            [
                pltpu.make_async_copy(src.at[:, at], dst.at[:, at], sems.at[group, i])
                for i, (src, dst) in enumerate(arrays)
            ]
        )
        for copy in copies[-1]:
            copy.start()
    cosine, sine = cos_ref[...], sin_ref[...]
    row = lax.broadcasted_iota(jnp.int32, (SPAN, 2 * SPAN), 0)
    col = lax.broadcasted_iota(jnp.int32, (SPAN, 2 * SPAN), 1) % SPAN
    lower = row >= col
    upper = row <= col
    for p in range(pairs):
        if p % GROUP == 0:
            for copy in copies[p // GROUP]:
                copy.wait()
        at = slice(p * PAIR, (p + 1) * PAIR)
        q = rotated(q_ref[:, at], cosine, sine).astype(BF16)
        k = rotated(k_ref[:, at], cosine, sine).astype(BF16)
        v, g = v_ref[:, at], g_ref[:, at]
        kr_ref[:, at] = k
        q2, k2, v2, g2 = by_head(q), by_head(k), by_head(v), by_head(g)
        w = jnp.where(lower, dot(g, v2, NT), 0.0).astype(BF16)
        wt = jnp.where(upper, dot(v, g2, NT), 0.0).astype(BF16)
        st = jnp.where(upper, dot(k, q2, NT), 0.0).astype(BF16)
        qo_ref[:, at] = dot(w, k2, NN)
        ko_ref[:, at] = dot(wt, q2, NN)
        vo_ref[:, at] = dot(st, g2, NN)


def chip_kernel(mine_ref, theirs_ref, *refs):
    block_in, out_ref, block = refs[:6], refs[6], refs[7:]
    core = lax.axis_index("core")
    for z in range(out_ref.shape[0]):
        out_ref[z] = (mine_ref[z] + theirs_ref[1 - core, z].astype(F32)).astype(BF16)

    @pl.when(core == 0)
    def _():
        block_products(*block_in, *block)


def totals_kernel(zr_ref, out_ref):
    state = zr_ref[0, 0].astype(F32)
    grad = zr_ref[0, 1].astype(F32)
    for z in range(1, zr_ref.shape[0]):
        state += zr_ref[z, 0].astype(F32)
        grad += zr_ref[z, 1].astype(F32)
    me = lax.axis_index("ctx")
    for j in range(out_ref.shape[0]):
        out_ref[j] = jnp.where(j > me, state, grad).astype(out_ref.dtype)


def scan_kernel(zr_ref, cx_ref, out_ref):
    me = lax.axis_index("ctx")
    state = jnp.zeros(cx_ref.shape[1:], F32)
    grad = jnp.zeros(cx_ref.shape[1:], F32)
    for j in range(cx_ref.shape[0]):
        state += jnp.where(j < me, cx_ref[j].astype(F32), 0.0)
        grad += jnp.where(j > me, cx_ref[j].astype(F32), 0.0)
    count = zr_ref.shape[0]
    for z in range(count):
        out_ref[z, 0] = state.astype(BF16)
        state += zr_ref[z, 0].astype(F32)
    for z in reversed(range(count)):
        out_ref[z, 1] = grad.astype(BF16)
        grad += zr_ref[z, 1].astype(F32)


def send_kernel(zb_ref, mine_ref, *refs):
    block_in, out_ref, block = refs[:6], refs[12], refs[13:]
    core = lax.axis_index("core")
    for z in range(zb_ref.shape[0]):
        out_ref[z, 0] = (zb_ref[z, 0].astype(F32) + jnp.where(core == 0, mine_ref[z, 0], 0.0)).astype(BF16)
        out_ref[z, 1] = (zb_ref[z, 1].astype(F32) + jnp.where(core == 1, mine_ref[z, 1], 0.0)).astype(BF16)

    @pl.when(core == 1)
    def _():
        block_products(*block_in, *block)


def finish_kernel(
    factor, k_ref, v_ref, g_ref, qi_ref, ki_ref, vi_ref, cos_ref, sin_ref, zb_ref, theirs_ref, sent_ref,
    q_out, k_out, v_out, qo_ref, ko_ref, vo_ref, out_sems,
):
    pairs = k_ref.shape[1] // PAIR
    core = lax.axis_index("core")
    other = 1 - core
    first = core * (pairs // 2)
    results = ((qo_ref, q_out), (ko_ref, k_out), (vo_ref, v_out))
    cosine, sine = cos_ref[...], -sin_ref[...]
    stores = []

    def carried(slot, kind):
        count = zb_ref.shape[0]
        if slot >= count:
            return sent_ref[other, slot - count, kind]
        near = theirs_ref[other, slot, kind].astype(F32)
        return (zb_ref[slot, kind].astype(F32) + jnp.where(core == 1 - kind, near, 0.0)).astype(BF16)

    for j in range(pairs):
        at = span(lax.rem(first + j, pairs))
        k, v, g = k_ref[:, at], v_ref[:, at], g_ref[:, at]
        before = by_head(jnp.concatenate([carried(2 * j, 0), carried(2 * j + 1, 0)], axis=0))
        after = by_head(jnp.concatenate([carried(2 * j, 1), carried(2 * j + 1, 1)], axis=0))
        qo = (factor * (qi_ref[:, at] + dot(g, before, NT))).astype(BF16)
        ko = (factor * (ki_ref[:, at] + dot(v, after, NT))).astype(BF16)
        vo_ref[:, at] = (factor * (vi_ref[:, at] + dot(k, after, NN))).astype(BF16)
        qo_ref[:, at] = rotated(qo, cosine, sine).astype(BF16)
        ko_ref[:, at] = rotated(ko, cosine, sine).astype(BF16)
        if j % GROUP == GROUP - 1:
            stores += store(results, out_sems, first, j // GROUP)
    for copy in stores:
        copy.wait()


VMEM = pl.BlockSpec(memory_space=pltpu.VMEM)
HBM = pl.BlockSpec(memory_space=pltpu.HBM)


def call(kernel, out_shape, *args, out_specs=VMEM, in_specs=None, scratch=(), aliases=None):
    in_specs = in_specs or [VMEM] * len(args)
    args = [pltpu.with_memory_space_constraint(x, spec.memory_space) for x, spec in zip(args, in_specs)]
    placed = jax.tree.map(lambda spec, x: spec.memory_space(x.shape, x.dtype), out_specs, out_shape)
    return pl.pallas_call(
        kernel,
        out_shape=placed,
        in_specs=in_specs,
        out_specs=out_specs,
        scratch_shapes=scratch,
        compiler_params=pltpu.CompilerParams(vmem_limit_bytes=VMEM_LIMIT),
        input_output_aliases=aliases or {},
    )(*args)


def on_device(query_rows, key_rows, value_rows, out_grad, positions):
    tokens, width = query_rows.shape
    n_ctx, n_z = lax.axis_size("ctx"), lax.axis_size("z")
    seq_total = tokens * n_ctx * n_z * lax.axis_size("core")
    factor = 1.0 / math.sqrt(HD * seq_total)
    pairs = width // PAIR
    groups = pairs // GROUP
    like = jax.ShapeDtypeStruct((tokens, width), BF16)
    wide = jax.ShapeDtypeStruct((tokens, width), F32)
    table = jax.ShapeDtypeStruct((tokens, PAIR), F32)
    half_low = jax.ShapeDtypeStruct((pairs, 2, HALF, PAIR), BF16)
    half_wide = jax.ShapeDtypeStruct((pairs, 2, HALF, PAIR), F32)

    low = pltpu.VMEM((tokens, width), BF16)
    rows = (query_rows, key_rows, value_rows, out_grad)
    cosine, sine, theirs, mine = call(
        states_kernel,
        [table] * 2 + [half_low, half_wide],
        positions.reshape(1, tokens), *rows,
        in_specs=[HBM] * 5,
        out_specs=[VMEM] * 4,
        scratch=[pltpu.VMEM((1, tokens), jnp.int32)]
        + [low] * 4
        + [pltpu.SemaphoreType.DMA((4,)), pltpu.SemaphoreType.DMA],
    )
    theirs = lax.all_gather(theirs, "core")
    block = [like] * 3 + [wide] * 3
    scratch = [low] * 2 + [pltpu.SemaphoreType.DMA((groups, 4))]
    chip, *inner = call(
        chip_kernel,
        [half_low] + block,
        mine, theirs, *rows, cosine, sine,
        in_specs=[VMEM] * 2 + [HBM] * 4 + [VMEM] * 2,
        out_specs=[VMEM] * 7,
        scratch=scratch,
    )
    over_z = lax.all_to_all(chip, "z", 0, 0, tiled=True)
    group = call(totals_kernel, jax.ShapeDtypeStruct((n_ctx, HALF, PAIR), BF16), over_z)
    over_ctx = lax.all_to_all(group, "ctx", 0, 0, tiled=True)
    sums = call(scan_kernel, half_low, over_z, over_ctx)
    back = lax.all_to_all(sums, "z", 0, 0, tiled=True)
    send, *inner = call(
        send_kernel,
        [half_low] + block,
        back, mine, *rows, cosine, sine, *inner,
        in_specs=[VMEM] * 2 + [HBM] * 4 + [VMEM] * 8,
        out_specs=[VMEM] * 7,
        scratch=scratch,
        aliases={8 + i: 1 + i for i in range(6)},
    )
    sent = lax.all_gather(send, "core")
    return call(
        functools.partial(finish_kernel, factor),
        [like] * 3,
        *inner, cosine, sine, back, theirs, sent,
        out_specs=[HBM] * 3,
        scratch=[low] * 3 + [pltpu.SemaphoreType.DMA((groups, 3))],
    )


def solution(mesh):
    split = Mesh(
        mesh.devices.reshape(mesh.shape["ctx"], mesh.shape["sp"] // 2, 2), ("ctx", "z", "core")
    )
    tokens = ("ctx", "z", "core")
    return jax.shard_map(
        on_device,
        mesh=split,
        in_specs=(P(tokens, None),) * 4 + (P(tokens),),
        out_specs=(P(tokens, None),) * 3,
        check_vma=False,
    )
```

```python
import functools
import math

import jax
import jax.numpy as jnp
from jax import lax
from jax.experimental import pallas as pl
from jax.experimental.pallas import tpu as pltpu
from jax.sharding import Mesh, PartitionSpec as P

HD = 64
SPAN = 128
BASE = 500000.0
PAIR = 2 * HD
HALF = HD // 2
F32 = jnp.float32
BF16 = jnp.bfloat16
GROUP = 4
VMEM_LIMIT = 16 * 1024 * 1024

NT = (((1,), (1,)), ((), ()))
TN = (((0,), (0,)), ((), ()))
NN = (((1,), (0,)), ((), ()))


def dot(a, b, dims):
    return lax.dot_general(a, b, dims, preferred_element_type=F32)


def lanes(rows):
    return lax.broadcasted_iota(jnp.int32, (rows, PAIR), 1)


def swap_halves(x):
    first = (lanes(x.shape[0]) % HD) < HALF
    return jnp.where(first, pltpu.roll(x, PAIR - HALF, 1), pltpu.roll(x, HALF, 1))


def swap_matrix():
    row = lax.broadcasted_iota(jnp.int32, (PAIR, PAIR), 0)
    lane = lanes(PAIR)
    source = jnp.where(lane % HD < HALF, lane + HALF, lane - HALF)
    return jnp.where(row == source, 1.0, 0.0).astype(BF16)


def rotated(x, cosine, sine):
    return x.astype(F32) * cosine + swap_halves(x).astype(F32) * sine


def by_head(x):
    first = lanes(x.shape[0]) < HD
    zero = jnp.zeros_like(x)
    return jnp.concatenate([jnp.where(first, x, zero), jnp.where(first, zero, x)], axis=0)


def pack_pair(m):
    first = lanes(HD) < HD
    return jnp.where(first, m[:HD], m[HD:])


def angle_tables(positions):
    index = lax.broadcasted_iota(jnp.int32, (HALF, positions.shape[1]), 0)
    frequency = jnp.ones(index.shape, F32)
    for bit in range(HALF.bit_length() - 1):
        part = BASE ** (-(2.0**bit) / HALF)
        frequency = jnp.where((index >> bit) % 2 == 1, frequency * part, frequency)
    angles = positions.astype(F32) * frequency
    cosine, sine = jnp.cos(angles), jnp.sin(angles)
    return (
        jnp.concatenate([cosine, cosine, cosine, cosine], axis=0).T,
        jnp.concatenate([-sine, sine, -sine, sine], axis=0).T,
    )


def span(first, count=1):
    return pl.ds(pl.multiple_of(first * PAIR, PAIR), count * PAIR)


def store(results, sems, first, group):
    pairs = results[0][0].shape[1] // PAIR
    at = span(lax.rem(first + group * GROUP, pairs), GROUP)
    copies = [
        pltpu.make_async_copy(src.at[:, at], dst.at[:, at], sems.at[group, i])
        for i, (src, dst) in enumerate(results)
    ]
    for copy in copies:
        copy.start()
    return copies


def states_kernel(
    pos_in, q_in, k_in, v_in, g_in,
    cos_ref, sin_ref, theirs_ref, mine_ref,
    pos_ref, q_ref, k_ref, v_ref, g_ref, sems, pos_sem,
):
    pairs = q_ref.shape[1] // PAIR
    first = (1 - lax.axis_index("core")) * (pairs // 2)
    pos_copy = pltpu.make_async_copy(pos_in, pos_ref, pos_sem)
    pos_copy.start()
    arrays = ((q_in, q_ref), (g_in, g_ref), (k_in, k_ref), (v_in, v_ref))
    copies = [pltpu.make_async_copy(src, dst, sems.at[i]) for i, (src, dst) in enumerate(arrays)]
    for copy in copies:
        copy.start()
    pos_copy.wait()
    cosine, sine = angle_tables(pos_ref[...])
    cos_ref[...] = cosine
    sin_ref[...] = sine
    swap = swap_matrix()
    for kind, left, right in ((1, q_ref, g_ref), (0, k_ref, v_ref)):
        copies[2 - 2 * kind].wait()
        copies[3 - 2 * kind].wait()
        for j in range(pairs):
            at = span(lax.rem(first + j, pairs))
            x = left[:, at]
            x = (x.astype(F32) * cosine + dot(x, swap, NN) * sine).astype(BF16)
            state = pack_pair(dot(x, right[:, at], TN))
            out, slot = (theirs_ref, 2 * j) if j < pairs // 2 else (mine_ref, 2 * j - pairs)
            for r in range(2):
                out[slot + r, kind] = state[HALF * r : HALF * (r + 1)].astype(out.dtype)


def block_products(
    q_in, k_in, v_in, g_in, cos_ref, sin_ref, kr_ref, v_ref, g_ref, qo_ref, ko_ref, vo_ref, q_ref, k_ref, sems
):
    pairs = q_ref.shape[1] // PAIR
    arrays = ((q_in, q_ref), (k_in, k_ref), (v_in, v_ref), (g_in, g_ref))
    copies = []
    for group in range(pairs // GROUP):
        at = slice(group * GROUP * PAIR, (group + 1) * GROUP * PAIR)
        copies.append(
            [
                pltpu.make_async_copy(src.at[:, at], dst.at[:, at], sems.at[group, i])
                for i, (src, dst) in enumerate(arrays)
            ]
        )
        for copy in copies[-1]:
            copy.start()
    cosine, sine = cos_ref[...], sin_ref[...]
    row = lax.broadcasted_iota(jnp.int32, (SPAN, 2 * SPAN), 0)
    col = lax.broadcasted_iota(jnp.int32, (SPAN, 2 * SPAN), 1) % SPAN
    lower = row >= col
    upper = row <= col
    for p in range(pairs):
        if p % GROUP == 0:
            for copy in copies[p // GROUP]:
                copy.wait()
        at = slice(p * PAIR, (p + 1) * PAIR)
        q = rotated(q_ref[:, at], cosine, sine).astype(BF16)
        k = rotated(k_ref[:, at], cosine, sine).astype(BF16)
        v, g = v_ref[:, at], g_ref[:, at]
        kr_ref[:, at] = k
        q2, k2, v2, g2 = by_head(q), by_head(k), by_head(v), by_head(g)
        w = jnp.where(lower, dot(g, v2, NT), 0.0).astype(BF16)
        wt = jnp.where(upper, dot(v, g2, NT), 0.0).astype(BF16)
        st = jnp.where(upper, dot(k, q2, NT), 0.0).astype(BF16)
        qo_ref[:, at] = dot(w, k2, NN)
        ko_ref[:, at] = dot(wt, q2, NN)
        vo_ref[:, at] = dot(st, g2, NN)


def chip_kernel(mine_ref, theirs_ref, *refs):
    block_in, out_ref, block = refs[:6], refs[6], refs[7:]
    core = lax.axis_index("core")
    for z in range(out_ref.shape[0]):
        out_ref[z] = (mine_ref[z] + theirs_ref[1 - core, z].astype(F32)).astype(BF16)

    @pl.when(core == 0)
    def _():
        block_products(*block_in, *block)


def z_members(count):
    middle = count // 2
    return [middle, middle - 1, *range(middle + 1, count), *range(middle - 2, -1, -1)]


def ctx_members(count):
    side = math.isqrt(count)

    def hops(i):
        return sum(min(at, side - at) for at in (i // side, i % side))

    return sorted(range(count), key=lambda i: (hops(i), i), reverse=True)


def totals_kernel(zr_ref, out_ref):
    state = zr_ref[0, 0].astype(F32)
    grad = zr_ref[0, 1].astype(F32)
    for z in range(1, zr_ref.shape[0]):
        state += zr_ref[z, 0].astype(F32)
        grad += zr_ref[z, 1].astype(F32)
    me = lax.axis_index("ctx")
    for slot, j in enumerate(ctx_members(out_ref.shape[0])):
        out_ref[slot] = jnp.where(j > me, state, grad).astype(out_ref.dtype)


def scan_kernel(zr_ref, cx_ref, out_ref):
    me = lax.axis_index("ctx")
    state = jnp.zeros(cx_ref.shape[1:], F32)
    grad = jnp.zeros(cx_ref.shape[1:], F32)
    for slot, j in enumerate(ctx_members(cx_ref.shape[0])):
        state += jnp.where(j < me, cx_ref[slot].astype(F32), 0.0)
        grad += jnp.where(j > me, cx_ref[slot].astype(F32), 0.0)
    order = z_members(zr_ref.shape[0])
    slots = [order.index(z) for z in range(len(order))]
    for at in slots:
        out_ref[at, 0] = state.astype(BF16)
        state += zr_ref[at, 0].astype(F32)
    for at in reversed(slots):
        out_ref[at, 1] = grad.astype(BF16)
        grad += zr_ref[at, 1].astype(F32)


def send_kernel(zb_ref, mine_ref, *refs):
    block_in, out_ref, block = refs[:6], refs[12], refs[13:]
    core = lax.axis_index("core")
    for z in range(zb_ref.shape[0]):
        out_ref[z, 0] = (zb_ref[z, 0].astype(F32) + jnp.where(core == 0, mine_ref[z, 0], 0.0)).astype(BF16)
        out_ref[z, 1] = (zb_ref[z, 1].astype(F32) + jnp.where(core == 1, mine_ref[z, 1], 0.0)).astype(BF16)

    @pl.when(core == 1)
    def _():
        block_products(*block_in, *block)


def finish_kernel(
    factor, k_ref, v_ref, g_ref, qi_ref, ki_ref, vi_ref, cos_ref, sin_ref, zb_ref, theirs_ref, sent_ref,
    q_out, k_out, v_out, qo_ref, ko_ref, vo_ref, out_sems,
):
    pairs = k_ref.shape[1] // PAIR
    core = lax.axis_index("core")
    other = 1 - core
    first = core * (pairs // 2)
    results = ((qo_ref, q_out), (ko_ref, k_out), (vo_ref, v_out))
    cosine, sine = cos_ref[...], -sin_ref[...]
    stores = []

    def carried(slot, kind):
        count = zb_ref.shape[0]
        if slot >= count:
            return sent_ref[other, slot - count, kind]
        near = theirs_ref[other, slot, kind].astype(F32)
        return (zb_ref[slot, kind].astype(F32) + jnp.where(core == 1 - kind, near, 0.0)).astype(BF16)

    for j in range(pairs):
        at = span(lax.rem(first + j, pairs))
        k, v, g = k_ref[:, at], v_ref[:, at], g_ref[:, at]
        before = by_head(jnp.concatenate([carried(2 * j, 0), carried(2 * j + 1, 0)], axis=0))
        after = by_head(jnp.concatenate([carried(2 * j, 1), carried(2 * j + 1, 1)], axis=0))
        qo = (factor * (qi_ref[:, at] + dot(g, before, NT))).astype(BF16)
        ko = (factor * (ki_ref[:, at] + dot(v, after, NT))).astype(BF16)
        vo_ref[:, at] = (factor * (vi_ref[:, at] + dot(k, after, NN))).astype(BF16)
        qo_ref[:, at] = rotated(qo, cosine, sine).astype(BF16)
        ko_ref[:, at] = rotated(ko, cosine, sine).astype(BF16)
        if j % GROUP == GROUP - 1:
            stores += store(results, out_sems, first, j // GROUP)
    for copy in stores:
        copy.wait()


VMEM = pl.BlockSpec(memory_space=pltpu.VMEM)
HBM = pl.BlockSpec(memory_space=pltpu.HBM)


def call(kernel, out_shape, *args, out_specs=VMEM, in_specs=None, scratch=(), aliases=None):
    in_specs = in_specs or [VMEM] * len(args)
    args = [pltpu.with_memory_space_constraint(x, spec.memory_space) for x, spec in zip(args, in_specs)]
    placed = jax.tree.map(lambda spec, x: spec.memory_space(x.shape, x.dtype), out_specs, out_shape)
    return pl.pallas_call(
        kernel,
        out_shape=placed,
        in_specs=in_specs,
        out_specs=out_specs,
        scratch_shapes=scratch,
        compiler_params=pltpu.CompilerParams(vmem_limit_bytes=VMEM_LIMIT),
        input_output_aliases=aliases or {},
    )(*args)


def on_device(query_rows, key_rows, value_rows, out_grad, positions):
    tokens, width = query_rows.shape
    n_ctx, n_z = lax.axis_size("ctx"), lax.axis_size("z")
    seq_total = tokens * n_ctx * n_z * lax.axis_size("core")
    factor = 1.0 / math.sqrt(HD * seq_total)
    pairs = width // PAIR
    groups = pairs // GROUP
    like = jax.ShapeDtypeStruct((tokens, width), BF16)
    wide = jax.ShapeDtypeStruct((tokens, width), F32)
    table = jax.ShapeDtypeStruct((tokens, PAIR), F32)
    half_low = jax.ShapeDtypeStruct((pairs, 2, HALF, PAIR), BF16)
    half_wide = jax.ShapeDtypeStruct((pairs, 2, HALF, PAIR), F32)

    low = pltpu.VMEM((tokens, width), BF16)
    rows = (query_rows, key_rows, value_rows, out_grad)
    cosine, sine, theirs, mine = call(
        states_kernel,
        [table] * 2 + [half_low, half_wide],
        positions.reshape(1, tokens), *rows,
        in_specs=[HBM] * 5,
        out_specs=[VMEM] * 4,
        scratch=[pltpu.VMEM((1, tokens), jnp.int32)]
        + [low] * 4
        + [pltpu.SemaphoreType.DMA((4,)), pltpu.SemaphoreType.DMA],
    )
    theirs = lax.all_gather(theirs, "core")
    block = [like] * 3 + [wide] * 3
    scratch = [low] * 2 + [pltpu.SemaphoreType.DMA((groups, 4))]
    chip, *inner = call(
        chip_kernel,
        [half_low] + block,
        mine, theirs, *rows, cosine, sine,
        in_specs=[VMEM] * 2 + [HBM] * 4 + [VMEM] * 2,
        out_specs=[VMEM] * 7,
        scratch=scratch,
    )
    over_z = lax.all_to_all(chip, "z", 0, 0, tiled=True, axis_index_groups=[z_members(n_z)])
    group = call(totals_kernel, jax.ShapeDtypeStruct((n_ctx, HALF, PAIR), BF16), over_z)
    over_ctx = lax.all_to_all(group, "ctx", 0, 0, tiled=True, axis_index_groups=[ctx_members(n_ctx)])
    sums = call(scan_kernel, half_low, over_z, over_ctx)
    back = lax.all_to_all(sums, "z", 0, 0, tiled=True, axis_index_groups=[z_members(n_z)])
    send, *inner = call(
        send_kernel,
        [half_low] + block,
        back, mine, *rows, cosine, sine, *inner,
        in_specs=[VMEM] * 2 + [HBM] * 4 + [VMEM] * 8,
        out_specs=[VMEM] * 7,
        scratch=scratch,
        aliases={8 + i: 1 + i for i in range(6)},
    )
    sent = lax.all_gather(send, "core")
    return call(
        functools.partial(finish_kernel, factor),
        [like] * 3,
        *inner, cosine, sine, back, theirs, sent,
        out_specs=[HBM] * 3,
        scratch=[low] * 3 + [pltpu.SemaphoreType.DMA((groups, 3))],
    )


def solution(mesh):
    split = Mesh(
        mesh.devices.reshape(mesh.shape["ctx"], mesh.shape["sp"] // 2, 2), ("ctx", "z", "core")
    )
    tokens = ("ctx", "z", "core")
    return jax.shard_map(
        on_device,
        mesh=split,
        in_specs=(P(tokens, None),) * 4 + (P(tokens),),
        out_specs=(P(tokens, None),) * 3,
        check_vma=False,
    )
```

```python
import functools
import math

import jax
import jax.numpy as jnp
from jax import lax
from jax.experimental import pallas as pl
from jax.experimental.pallas import tpu as pltpu
from jax.sharding import Mesh, PartitionSpec as P

HD = 64
SPAN = 128
BASE = 500000.0
PAIR = 2 * HD
HALF = HD // 2
F32 = jnp.float32
BF16 = jnp.bfloat16
GROUP = 4
VMEM_LIMIT = 16 * 1024 * 1024

NT = (((1,), (1,)), ((), ()))
TN = (((0,), (0,)), ((), ()))
NN = (((1,), (0,)), ((), ()))


def dot(a, b, dims):
    return lax.dot_general(a, b, dims, preferred_element_type=F32)


def lanes(rows):
    return lax.broadcasted_iota(jnp.int32, (rows, PAIR), 1)


def swap_halves(x):
    first = (lanes(x.shape[0]) % HD) < HALF
    return jnp.where(first, pltpu.roll(x, PAIR - HALF, 1), pltpu.roll(x, HALF, 1))


def swap_matrix():
    row = lax.broadcasted_iota(jnp.int32, (PAIR, PAIR), 0)
    lane = lanes(PAIR)
    source = jnp.where(lane % HD < HALF, lane + HALF, lane - HALF)
    return jnp.where(row == source, 1.0, 0.0).astype(BF16)


def rotated(x, cosine, sine):
    return x.astype(F32) * cosine + swap_halves(x).astype(F32) * sine


def by_head(x):
    first = lanes(x.shape[0]) < HD
    zero = jnp.zeros_like(x)
    return jnp.concatenate([jnp.where(first, x, zero), jnp.where(first, zero, x)], axis=0)


def pack_pair(m):
    first = lanes(HD) < HD
    return jnp.where(first, m[:HD], m[HD:])


def angle_tables(positions):
    index = lax.broadcasted_iota(jnp.int32, (HALF, positions.shape[1]), 0)
    frequency = jnp.ones(index.shape, F32)
    for bit in range(HALF.bit_length() - 1):
        part = BASE ** (-(2.0**bit) / HALF)
        frequency = jnp.where((index >> bit) % 2 == 1, frequency * part, frequency)
    angles = positions.astype(F32) * frequency
    cosine, sine = jnp.cos(angles), jnp.sin(angles)
    return (
        jnp.concatenate([cosine, cosine, cosine, cosine], axis=0).T,
        jnp.concatenate([-sine, sine, -sine, sine], axis=0).T,
    )


def span(first, count=1):
    return pl.ds(pl.multiple_of(first * PAIR, PAIR), count * PAIR)


def store(results, sems, first, group):
    pairs = results[0][0].shape[1] // PAIR
    at = span(lax.rem(first + group * GROUP, pairs), GROUP)
    copies = [
        pltpu.make_async_copy(src.at[:, at], dst.at[:, at], sems.at[group, i])
        for i, (src, dst) in enumerate(results)
    ]
    for copy in copies:
        copy.start()
    return copies


def states_kernel(
    pos_in, q_in, k_in, v_in, g_in,
    cos_ref, sin_ref, theirs_ref, mine_ref,
    pos_ref, q_ref, k_ref, v_ref, g_ref, sems, pos_sem,
):
    pairs = q_ref.shape[1] // PAIR
    first = (1 - lax.axis_index("core")) * (pairs // 2)
    pos_copy = pltpu.make_async_copy(pos_in, pos_ref, pos_sem)
    pos_copy.start()
    arrays = ((q_in, q_ref), (g_in, g_ref), (k_in, k_ref), (v_in, v_ref))
    copies = [pltpu.make_async_copy(src, dst, sems.at[i]) for i, (src, dst) in enumerate(arrays)]
    for copy in copies:
        copy.start()
    pos_copy.wait()
    cosine, sine = angle_tables(pos_ref[...])
    cos_ref[...] = cosine
    sin_ref[...] = sine
    swap = swap_matrix()
    for kind, left, right in ((1, q_ref, g_ref), (0, k_ref, v_ref)):
        copies[2 - 2 * kind].wait()
        copies[3 - 2 * kind].wait()
        for j in range(pairs):
            at = span(lax.rem(first + j, pairs))
            x = left[:, at]
            x = (x.astype(F32) * cosine + dot(x, swap, NN) * sine).astype(BF16)
            state = pack_pair(dot(x, right[:, at], TN))
            out, slot = (theirs_ref, 2 * j) if j < pairs // 2 else (mine_ref, 2 * j - pairs)
            for r in range(2):
                out[slot + r, kind] = state[HALF * r : HALF * (r + 1)].astype(out.dtype)


def block_products(
    q_in, k_in, v_in, g_in, cos_ref, sin_ref, kr_ref, v_ref, g_ref, qo_ref, ko_ref, vo_ref, q_ref, k_ref, sems
):
    pairs = q_ref.shape[1] // PAIR
    arrays = ((q_in, q_ref), (k_in, k_ref), (v_in, v_ref), (g_in, g_ref))
    copies = []
    for group in range(pairs // GROUP):
        at = slice(group * GROUP * PAIR, (group + 1) * GROUP * PAIR)
        copies.append(
            [
                pltpu.make_async_copy(src.at[:, at], dst.at[:, at], sems.at[group, i])
                for i, (src, dst) in enumerate(arrays)
            ]
        )
        for copy in copies[-1]:
            copy.start()
    cosine, sine = cos_ref[...], sin_ref[...]
    row = lax.broadcasted_iota(jnp.int32, (SPAN, 2 * SPAN), 0)
    col = lax.broadcasted_iota(jnp.int32, (SPAN, 2 * SPAN), 1) % SPAN
    lower = row >= col
    upper = row <= col
    for p in range(pairs):
        if p % GROUP == 0:
            for copy in copies[p // GROUP]:
                copy.wait()
        at = slice(p * PAIR, (p + 1) * PAIR)
        q = rotated(q_ref[:, at], cosine, sine).astype(BF16)
        k = rotated(k_ref[:, at], cosine, sine).astype(BF16)
        v, g = v_ref[:, at], g_ref[:, at]
        kr_ref[:, at] = k
        q2, k2, v2, g2 = by_head(q), by_head(k), by_head(v), by_head(g)
        w = jnp.where(lower, dot(g, v2, NT), 0.0).astype(BF16)
        wt = jnp.where(upper, dot(v, g2, NT), 0.0).astype(BF16)
        st = jnp.where(upper, dot(k, q2, NT), 0.0).astype(BF16)
        qo_ref[:, at] = dot(w, k2, NN)
        ko_ref[:, at] = dot(wt, q2, NN)
        vo_ref[:, at] = dot(st, g2, NN)


def chip_kernel(mine_ref, theirs_ref, *refs):
    block_in, out_ref, block = refs[:6], refs[6], refs[7:]
    core = lax.axis_index("core")
    for z in range(out_ref.shape[0]):
        out_ref[z] = (mine_ref[z] + theirs_ref[1 - core, z].astype(F32)).astype(BF16)

    @pl.when(core == 0)
    def _():
        block_products(*block_in, *block)


def z_members(count):
    middle = count // 2
    return [middle, middle - 1, *range(middle + 1, count), *range(middle - 2, -1, -1)]


def ctx_members(count):
    side = math.isqrt(count)

    def hops(i):
        return sum(min(at, side - at) for at in (i // side, i % side))

    return sorted(range(count), key=lambda i: (hops(i), i % side, i), reverse=True)


def totals_kernel(zr_ref, out_ref):
    state = zr_ref[0, 0].astype(F32)
    grad = zr_ref[0, 1].astype(F32)
    for z in range(1, zr_ref.shape[0]):
        state += zr_ref[z, 0].astype(F32)
        grad += zr_ref[z, 1].astype(F32)
    me = lax.axis_index("ctx")
    for slot, j in enumerate(ctx_members(out_ref.shape[0])):
        out_ref[slot] = jnp.where(j > me, state, grad).astype(out_ref.dtype)


def scan_kernel(zr_ref, cx_ref, out_ref):
    me = lax.axis_index("ctx")
    state = jnp.zeros(cx_ref.shape[1:], F32)
    grad = jnp.zeros(cx_ref.shape[1:], F32)
    for slot, j in enumerate(ctx_members(cx_ref.shape[0])):
        state += jnp.where(j < me, cx_ref[slot].astype(F32), 0.0)
        grad += jnp.where(j > me, cx_ref[slot].astype(F32), 0.0)
    order = z_members(zr_ref.shape[0])
    slots = [order.index(z) for z in range(len(order))]
    for at in slots:
        out_ref[at, 0] = state.astype(BF16)
        state += zr_ref[at, 0].astype(F32)
    for at in reversed(slots):
        out_ref[at, 1] = grad.astype(BF16)
        grad += zr_ref[at, 1].astype(F32)


def send_kernel(zb_ref, mine_ref, *refs):
    block_in, out_ref, block = refs[:6], refs[12], refs[13:]
    core = lax.axis_index("core")
    for z in range(zb_ref.shape[0]):
        out_ref[z, 0] = (zb_ref[z, 0].astype(F32) + jnp.where(core == 0, mine_ref[z, 0], 0.0)).astype(BF16)
        out_ref[z, 1] = (zb_ref[z, 1].astype(F32) + jnp.where(core == 1, mine_ref[z, 1], 0.0)).astype(BF16)

    @pl.when(core == 1)
    def _():
        block_products(*block_in, *block)


def finish_kernel(
    factor, k_ref, v_ref, g_ref, qi_ref, ki_ref, vi_ref, cos_ref, sin_ref, zb_ref, theirs_ref, sent_ref,
    q_out, k_out, v_out, qo_ref, ko_ref, vo_ref, out_sems,
):
    pairs = k_ref.shape[1] // PAIR
    core = lax.axis_index("core")
    other = 1 - core
    first = core * (pairs // 2)
    results = ((qo_ref, q_out), (ko_ref, k_out), (vo_ref, v_out))
    cosine, sine = cos_ref[...], -sin_ref[...]
    stores = []

    def carried(slot, kind):
        count = zb_ref.shape[0]
        if slot >= count:
            return sent_ref[other, slot - count, kind]
        near = theirs_ref[other, slot, kind].astype(F32)
        return (zb_ref[slot, kind].astype(F32) + jnp.where(core == 1 - kind, near, 0.0)).astype(BF16)

    for j in range(pairs):
        at = span(lax.rem(first + j, pairs))
        k, v, g = k_ref[:, at], v_ref[:, at], g_ref[:, at]
        before = by_head(jnp.concatenate([carried(2 * j, 0), carried(2 * j + 1, 0)], axis=0))
        after = by_head(jnp.concatenate([carried(2 * j, 1), carried(2 * j + 1, 1)], axis=0))
        qo = (factor * (qi_ref[:, at] + dot(g, before, NT))).astype(BF16)
        ko = (factor * (ki_ref[:, at] + dot(v, after, NT))).astype(BF16)
        vo_ref[:, at] = (factor * (vi_ref[:, at] + dot(k, after, NN))).astype(BF16)
        qo_ref[:, at] = rotated(qo, cosine, sine).astype(BF16)
        ko_ref[:, at] = rotated(ko, cosine, sine).astype(BF16)
        if j % GROUP == GROUP - 1:
            stores += store(results, out_sems, first, j // GROUP)
    for copy in stores:
        copy.wait()


VMEM = pl.BlockSpec(memory_space=pltpu.VMEM)
HBM = pl.BlockSpec(memory_space=pltpu.HBM)


def call(kernel, out_shape, *args, out_specs=VMEM, in_specs=None, scratch=(), aliases=None):
    in_specs = in_specs or [VMEM] * len(args)
    args = [pltpu.with_memory_space_constraint(x, spec.memory_space) for x, spec in zip(args, in_specs)]
    placed = jax.tree.map(lambda spec, x: spec.memory_space(x.shape, x.dtype), out_specs, out_shape)
    return pl.pallas_call(
        kernel,
        out_shape=placed,
        in_specs=in_specs,
        out_specs=out_specs,
        scratch_shapes=scratch,
        compiler_params=pltpu.CompilerParams(vmem_limit_bytes=VMEM_LIMIT),
        input_output_aliases=aliases or {},
    )(*args)


def on_device(query_rows, key_rows, value_rows, out_grad, positions):
    tokens, width = query_rows.shape
    n_ctx, n_z = lax.axis_size("ctx"), lax.axis_size("z")
    seq_total = tokens * n_ctx * n_z * lax.axis_size("core")
    factor = 1.0 / math.sqrt(HD * seq_total)
    pairs = width // PAIR
    groups = pairs // GROUP
    like = jax.ShapeDtypeStruct((tokens, width), BF16)
    wide = jax.ShapeDtypeStruct((tokens, width), F32)
    table = jax.ShapeDtypeStruct((tokens, PAIR), F32)
    half_low = jax.ShapeDtypeStruct((pairs, 2, HALF, PAIR), BF16)
    half_wide = jax.ShapeDtypeStruct((pairs, 2, HALF, PAIR), F32)

    low = pltpu.VMEM((tokens, width), BF16)
    rows = (query_rows, key_rows, value_rows, out_grad)
    cosine, sine, theirs, mine = call(
        states_kernel,
        [table] * 2 + [half_low, half_wide],
        positions.reshape(1, tokens), *rows,
        in_specs=[HBM] * 5,
        out_specs=[VMEM] * 4,
        scratch=[pltpu.VMEM((1, tokens), jnp.int32)]
        + [low] * 4
        + [pltpu.SemaphoreType.DMA((4,)), pltpu.SemaphoreType.DMA],
    )
    theirs = lax.all_gather(theirs, "core")
    block = [like] * 3 + [wide] * 3
    scratch = [low] * 2 + [pltpu.SemaphoreType.DMA((groups, 4))]
    chip, *inner = call(
        chip_kernel,
        [half_low] + block,
        mine, theirs, *rows, cosine, sine,
        in_specs=[VMEM] * 2 + [HBM] * 4 + [VMEM] * 2,
        out_specs=[VMEM] * 7,
        scratch=scratch,
    )
    over_z = lax.all_to_all(chip, "z", 0, 0, tiled=True, axis_index_groups=[z_members(n_z)])
    group = call(totals_kernel, jax.ShapeDtypeStruct((n_ctx, HALF, PAIR), BF16), over_z)
    over_ctx = lax.all_to_all(group, "ctx", 0, 0, tiled=True, axis_index_groups=[ctx_members(n_ctx)])
    sums = call(scan_kernel, half_low, over_z, over_ctx)
    back = lax.all_to_all(sums, "z", 0, 0, tiled=True, axis_index_groups=[z_members(n_z)])
    send, *inner = call(
        send_kernel,
        [half_low] + block,
        back, mine, *rows, cosine, sine, *inner,
        in_specs=[VMEM] * 2 + [HBM] * 4 + [VMEM] * 8,
        out_specs=[VMEM] * 7,
        scratch=scratch,
        aliases={8 + i: 1 + i for i in range(6)},
    )
    sent = lax.all_gather(send, "core")
    return call(
        functools.partial(finish_kernel, factor),
        [like] * 3,
        *inner, cosine, sine, back, theirs, sent,
        out_specs=[HBM] * 3,
        scratch=[low] * 3 + [pltpu.SemaphoreType.DMA((groups, 3))],
    )


def solution(mesh):
    split = Mesh(
        mesh.devices.reshape(mesh.shape["ctx"], mesh.shape["sp"] // 2, 2), ("ctx", "z", "core")
    )
    tokens = ("ctx", "z", "core")
    return jax.shard_map(
        on_device,
        mesh=split,
        in_specs=(P(tokens, None),) * 4 + (P(tokens),),
        out_specs=(P(tokens, None),) * 3,
        check_vma=False,
    )
```
